128 devices in a mesh: dp: 128 (over y, z, x, core).
Axes of the slice: x: 4, y: 4, z: 4, core: 2. Of those that a mesh axis runs over, the one named last changes fastest.
Arguments:
- grads: bfloat16 [1152, 7168], P('dp'), may hold values from -60 to 60
- momentum_slots: float32 [384, 56, 1152], P('dp'), may hold values from -60 to 60
- table: int32 [128], replicated, may hold values from 0 to 127, as said below
Outputs:
- update: bfloat16 [1152, 7168], replicated
- new_momentum: float32 [384, 56, 1152], P('dp')
The draws below stay inside these ranges and needn't reach their ends.
Inputs may be any that keep to these rules, and one draw needn't show every extreme that they name: `table`: no device owns more than 3 blocks, and some device owns exactly 3.
All inputs are finite; a program needn't handle non-finite values.
Results may differ from the reference program's by a relative error of at most 0.001.
Values may be sent and summed in bfloat16 or wider, within the bound.
A program may use at most 512 MiB of HBM per device.

```python
import math
import jax
import jax.numpy as jnp
from jax import lax

R = 576
C = 7168
LAYERS = 2
ITERS = 5
BLOCKS = 128
ROWS = 1152
CBW = 56
MOST = 3
SLOTS = 384
N_DP = 128


def spread_scales(key, count, spread):
    return jnp.exp(jax.random.uniform(key, (count,), jnp.float32, 0.0, math.log(spread)))


def draw_table(key, part):
    key = jax.random.fold_in(key, 11)
    key_heavy, key_slots, key_blocks = jax.random.split(key, 3)
    heavy = jax.random.randint(key_heavy, (), 0, N_DP)
    slot_ids = jnp.arange(SLOTS, dtype=jnp.int32)
    owners_of_slot = slot_ids // MOST
    shuffled = jax.random.permutation(key_slots, SLOTS)
    priority = jnp.zeros((SLOTS,), jnp.int32).at[shuffled].set(slot_ids)
    priority = jnp.where(owners_of_slot == heavy, slot_ids % MOST - SLOTS, priority)
    chosen = jnp.argsort(priority, stable=True)[:BLOCKS]
    owner_list = owners_of_slot[chosen]
    block_order = jax.random.permutation(key_blocks, BLOCKS)
    return jnp.zeros((BLOCKS,), jnp.int32).at[block_order].set(owner_list)


def draw_grads(key, part):
    key = jax.random.fold_in(key, 12)
    key_base, key_rows, key_cols = jax.random.split(key, 3)
    base = jnp.clip(jax.random.normal(key_base, (ROWS, C), jnp.float32), -4.0, 4.0)
    values = base * spread_scales(key_rows, ROWS, 3.16)[:, None] * spread_scales(key_cols, C, 3.16)[None, :]
    return values.astype(jnp.bfloat16)


def draw_momentum_slots(key, part):
    key = jax.random.fold_in(key, 13)
    key_base, key_rows, key_cols = jax.random.split(key, 3)
    base = jnp.clip(jax.random.normal(key_base, (SLOTS, CBW, ROWS), jnp.float32), -4.0, 4.0)
    column_scale = spread_scales(key_cols, SLOTS * CBW, 3.16).reshape(SLOTS, CBW, 1)
    values = base * column_scale * spread_scales(key_rows, ROWS, 3.16)[None, None, :]
    return values


def setup_inputs(seed: int = 0) -> dict:
    arg_keys = jax.random.split(jax.random.key(seed), 4)
    return {
        "grads": draw_grads(jax.random.fold_in(arg_keys[3], 71), 0),
        "momentum_slots": draw_momentum_slots(jax.random.fold_in(arg_keys[3], 71), 0),
        "table": draw_table(jax.random.fold_in(arg_keys[3], 71), 0),
    }


coef_a = 3.4445
coef_b = -4.775
coef_c = 2.0315
epsilon = 1e-07

def slot_of_blocks(table, slot_count):
    positions = jnp.arange(table.shape[0], dtype=jnp.int32)
    matching = (table[None, :] == table[:, None]) & (positions[None, :] < positions[:, None])
    ranking = lax.optimization_barrier(jnp.sum(matching.astype(jnp.int32), axis=1)).astype(jnp.int32)
    return (table * slot_count + ranking).astype(jnp.int32)

def reference(grads, momentum_slots, table):
    slot_index = slot_of_blocks(table, MOST)
    previous = jnp.take(momentum_slots, slot_index, axis=0)
    transposed = grads.astype(jnp.float32).reshape(ROWS, BLOCKS, CBW).transpose(1, 2, 0)
    refreshed = 0.95 * previous + transposed
    new_momentum = jnp.zeros((SLOTS, CBW, ROWS), jnp.float32).at[slot_index].set(refreshed)
    stacked = refreshed.transpose(2, 0, 1).reshape(LAYERS, R, C)
    frob_norm = jnp.sqrt(lax.optimization_barrier(jnp.sum(stacked * stacked, axis=(1, 2))))
    current = stacked / (frob_norm + epsilon)[:, None, None]
    for sweep in range(ITERS):
        gram_mat = jnp.einsum('mrc,msc->mrs', current, current, precision=lax.Precision.HIGHEST)
        squared = jnp.einsum('mrs,mst->mrt', gram_mat, gram_mat, precision=lax.Precision.HIGHEST)
        poly_mat = coef_b * gram_mat + coef_c * squared
        current = coef_a * current + jnp.einsum('mrs,msc->mrc', poly_mat, current, precision=lax.Precision.HIGHEST)
    rms_factor = 0.2 * math.sqrt(max(R, C))
    update = (rms_factor * current).reshape(ROWS, C).astype(jnp.bfloat16)
    return (update, new_momentum)
```

```python
import math

import jax
import jax.numpy as jnp
from jax import lax
from jax.sharding import PartitionSpec as P

R = 576
C = 7168
ITERS = 5


coef_a = 3.4445
coef_b = -4.775
coef_c = 2.0315
epsilon = 1e-07


def slot_of_blocks(table, slot_count):
    positions = jnp.arange(table.shape[0], dtype=jnp.int32)
    matching = (table[None, :] == table[:, None]) & (positions[None, :] < positions[:, None])
    ranking = jnp.sum(matching.astype(jnp.int32), axis=1)
    return table * slot_count + ranking


def gram_sum(values):
    partial_gram = jnp.einsum("jcmr,jcms->mrs", values, values, precision=lax.Precision.HIGHEST)
    return lax.psum(partial_gram, "dp")


def quintic(gram_mat):
    squared = jnp.matmul(gram_mat, gram_mat, precision=lax.Precision.HIGHEST)
    return coef_b * gram_mat + coef_c * squared


def apply_poly(values, poly_mat):
    return jnp.einsum("jcms,mrs->jcmr", values, poly_mat, precision=lax.Precision.HIGHEST)


def local(grads, momentum_slots, table):
    devices = lax.axis_size("dp")
    my_index = lax.axis_index("dp")
    row_dev = grads.shape[0]
    full_width = grads.shape[1]
    slot_count = momentum_slots.shape[0]
    block_width = momentum_slots.shape[1]
    rows_all = momentum_slots.shape[2]
    block_total = full_width // block_width
    layers = rows_all // R
    slots_all = devices * slot_count
    slot_index = slot_of_blocks(table, slot_count)
    hits = slot_index[None, :] == jnp.arange(slots_all, dtype=jnp.int32)[:, None]
    occupied = jnp.any(hits, axis=1)
    block_of = jnp.sum(
        jnp.where(hits, jnp.arange(block_total, dtype=jnp.int32)[None, :], 0), axis=1
    )
    pieces = grads.reshape(row_dev, block_total, block_width).transpose(1, 2, 0)
    outgoing = jnp.take(pieces, block_of, axis=0) * occupied[:, None, None].astype(jnp.bfloat16)
    outgoing = outgoing.reshape(devices, slot_count, block_width, row_dev)
    arrived = lax.all_to_all(outgoing, "dp", split_axis=0, concat_axis=3, tiled=True)
    arrived = arrived.reshape(slot_count, block_width, rows_all)
    mine = lax.dynamic_slice_in_dim(occupied, my_index * slot_count, slot_count)
    refreshed = (0.95 * momentum_slots + arrived.astype(jnp.float32)) * mine[:, None, None].astype(
        jnp.float32
    )
    per_layer = refreshed.reshape(slot_count, block_width, layers, R)
    gram_raw = gram_sum(per_layer)
    frob_norm = jnp.sqrt(jnp.trace(gram_raw, axis1=1, axis2=2))
    inverse = 1.0 / (frob_norm + epsilon)
    gram_mat = gram_raw * (inverse * inverse)[:, None, None]
    eye = jnp.eye(R, dtype=jnp.float32)
    current = per_layer * inverse[None, None, :, None]
    for sweep in range(ITERS):
        poly_mat = coef_a * eye + quintic(gram_mat)
        current = apply_poly(current, poly_mat)
        if sweep < ITERS - 1:
            half = jnp.matmul(poly_mat, gram_mat, precision=lax.Precision.HIGHEST)
            gram_mat = jnp.matmul(half, poly_mat, precision=lax.Precision.HIGHEST)
    rms_factor = 0.2 * math.sqrt(max(R, C))
    scaled = (rms_factor * current).reshape(slot_count, block_width, rows_all).astype(jnp.bfloat16)
    going_back = scaled.reshape(slot_count, block_width, devices, row_dev)
    returned = lax.all_to_all(going_back, "dp", split_axis=2, concat_axis=0, tiled=True)
    returned = returned.reshape(slots_all, block_width, row_dev)
    ordered = jnp.take(returned, slot_index, axis=0).transpose(2, 0, 1).reshape(row_dev, full_width)
    update = lax.all_gather(ordered, "dp", axis=0, tiled=True)
    return (update, refreshed)


def solution(mesh):
    in_specs = (P("dp", None), P("dp", None, None), P())
    out_specs = (P(), P("dp", None, None))
    return jax.shard_map(local, mesh=mesh, in_specs=in_specs, out_specs=out_specs, check_vma=False)
```

```python
import math

import jax
import jax.numpy as jnp
from jax import lax
from jax.experimental import pallas as pl
from jax.experimental.pallas import tpu as pltpu
from jax.sharding import PartitionSpec as P

R = 576
ITERS = 5
RP = 640
DEVICES = 128
CHIPS = 64
CORES_TILES = 35
MESH = pl.DeviceIdType.MESH
F32 = jnp.float32
BF16 = jnp.bfloat16

coef_a = 3.4445
coef_b = -4.775
coef_c = 2.0315
epsilon = 1e-07


def position():
    me = lax.axis_index("dp")
    return me, me // 2, lax.rem(me, 2)


def remote(src, dst, send, recv, to):
    return pltpu.make_async_remote_copy(
        src, dst, send, recv, device_id=(to,), device_id_type=MESH
    )


def drain(view, sem):
    pltpu.make_async_copy(view, view, sem).wait()


def greet_all(me):
    barrier = pltpu.get_barrier_semaphore()

    def greet(i, carry):
        pl.semaphore_signal(
            barrier, inc=1, device_id=(jnp.bitwise_xor(me, i),), device_id_type=MESH
        )
        return carry

    lax.fori_loop(1, DEVICES, greet, 0)
    pl.semaphore_wait(barrier, DEVICES - 1)


def split(value):
    high = value.astype(BF16)
    return high, (value - high.astype(F32)).astype(BF16)


def dot(a, b):
    return jnp.dot(a, b, preferred_element_type=F32)


def window_start(t):
    return min(128 * t // 9, DEVICES - 16)


def scatter_kernel(out_ref, mom_ref, mine_ref, fresh_ref, got, place, send, recv):
    me, _, _ = position()
    greet_all(me)

    def push(i, carry):
        to = jnp.bitwise_xor(me, i)
        remote(out_ref.at[to], got.at[me], send, recv, to).start()
        return carry

    lax.fori_loop(1, DEVICES, push, 0)
    got[pl.ds(me, 1)] = out_ref[pl.ds(me, 1)]
    rows = lax.broadcasted_iota(jnp.int32, (256, 128), 0)
    lanes = lax.broadcasted_iota(jnp.int32, (1, 128), 1)
    for t in range(9):
        line = lanes + 128 * t
        source = lax.shift_right_logical(line * 7282, 16)
        r = line - 9 * source
        half = lax.shift_right_logical(r, 1)
        odd = r - 2 * half
        base = 16 * (source - window_start(t)) + half
        for k in range(3):
            for parity in range(2):
                target = jnp.where(odd == parity, base + 5 * k, -1)
                place[t, :, pl.ds(128 * (2 * k + parity), 128)] = jnp.where(
                    rows == target, 1.0, 0.0
                ).astype(BF16)
    others = got.at[pl.ds(0, DEVICES - 1)]
    drain(others, recv)
    for t in range(9):
        window = got[pl.ds(window_start(t), 16)].reshape(256, 128)
        placed = lax.dot_general(
            window, place[t], (((0,), (0,)), ((), ())), preferred_element_type=F32
        )
        for k in range(3):
            arrived = (
                placed[0:56, 256 * k : 256 * k + 128]
                + placed[64:120, 256 * k + 128 : 256 * k + 256]
            )
            fresh_ref[k, :, pl.ds(128 * t, 128)] = (
                0.95 * mom_ref[k, :, pl.ds(128 * t, 128)] + arrived
            ) * mine_ref[k]
    drain(others, send)


def scatter(outgoing, momentum, mine):
    return pl.pallas_call(
        scatter_kernel,
        out_shape=jax.ShapeDtypeStruct(momentum.shape, F32),
        in_specs=[
            pl.BlockSpec(memory_space=pltpu.VMEM),
            pl.BlockSpec(memory_space=pltpu.VMEM),
            pl.BlockSpec(memory_space=pltpu.SMEM),
        ],
        out_specs=pl.BlockSpec(memory_space=pltpu.VMEM),
        scratch_shapes=[
            pltpu.VMEM((DEVICES, 16, 128), BF16),
            pltpu.VMEM((9, 256, 768), BF16),
            pltpu.SemaphoreType.DMA,
            pltpu.SemaphoreType.DMA,
        ],
        compiler_params=pltpu.CompilerParams(
            collective_id=0, has_side_effects=True, vmem_limit_bytes=40 * 2**20
        ),
        name="scatter",
    )(outgoing, momentum, mine)


def align_layer(value, core):
    moved = pltpu.roll(value, (RP - 64) * core, 1)
    lane = lax.broadcasted_iota(jnp.int32, value.shape, 1)
    return jnp.where(lane < R, moved, 0.0)


STRIP = (0, 576, 1024, 1344)


def pack(gram, packed):
    lane = lax.broadcasted_iota(jnp.int32, (64, 128), 1)
    corner = pltpu.roll(gram[512:576, 512:640], 64, 1)
    packed[0:64, :] = jnp.where(lane < 64, gram[0:64, 0:128], corner)
    packed[64:576, :] = gram[64:576, 0:128]
    for s in range(1, 4):
        packed[STRIP[s] : STRIP[s] + 576 - 128 * s, :] = gram[
            128 * s : 576, 128 * s : 128 * s + 128
        ]


def unpack(packed, gram):
    row = lax.broadcasted_iota(jnp.int32, (128, 128), 0)
    lane = lax.broadcasted_iota(jnp.int32, (128, 128), 1)
    upper = (row < 64) & (lane >= 64)
    first = packed[0:128, :]
    clean = jnp.where(upper, 0.0, first)
    gram[0:128, 0:128] = jnp.where(upper, clean.T, clean)
    corner = pltpu.roll(packed[0:64, :], 64, 1)
    lane64 = lax.broadcasted_iota(jnp.int32, (64, 128), 1)
    gram[512:576, 512:640] = jnp.where(lane64 < 64, corner, 0.0)
    gram[576:640, :] = jnp.zeros((64, RP), F32)
    for s in range(4):
        for b in range(s, 5):
            if b == s:
                if s:
                    gram[128 * s : 128 * s + 128, 128 * s : 128 * s + 128] = packed[
                        STRIP[s] : STRIP[s] + 128, :
                    ]
                continue
            n = 64 if b == 4 else 128
            start = STRIP[s] + 128 * (b - s)
            block = packed[start : start + n, :]
            gram[128 * b : 128 * b + n, 128 * s : 128 * s + 128] = block
            if n == 64:
                block = jnp.concatenate([block, jnp.zeros((64, 128), F32)], axis=0)
            gram[128 * s : 128 * s + 128, 128 * b : 128 * b + 128] = block.T


def left_form(value, ref):
    high, low = split(value)
    ref[:, 0:RP] = high
    ref[:, RP : 2 * RP] = high
    ref[:, 2 * RP : 3 * RP] = low


def right_form(value, ref):
    high, low = split(value)
    ref[0:RP, :] = high
    ref[RP : 2 * RP, :] = low
    ref[2 * RP : 3 * RP, :] = high


def iterate_kernel(
    fresh_ref, slot_ref, tile_ref,
    columns, packed, terms, summed, relay, chosen, mcol, gram, ga, gb, pb, ta, xa,
    swap_send, swap_recv, rs_send, rs_recv, ag_send, ag_recv, h1_send, h1_recv, h2_send, h2_recv,
):
    me, chip, core = position()
    greet_all(me)
    sibling = chip * 2 + 1 - core
    mine_lanes = pl.ds(pl.multiple_of(512 * core, 128), RP)
    their_lanes = pl.ds(pl.multiple_of(512 * (1 - core), 128), RP)
    swap = remote(fresh_ref.at[:, :, their_lanes], columns.at[1], swap_send, swap_recv, sibling)
    swap.start()

    def to_relay(i, carry):
        layer = i // CORES_TILES
        u = lax.rem(i, CORES_TILES)
        t = u // 7 + 4 * layer
        q = lax.rem(u, 7)
        to = jnp.where(layer == 0, u * 2 + 1, (63 - u) * 2)
        src = fresh_ref.at[:, pl.ds(pl.multiple_of(8 * q, 8), 8), pl.ds(pl.multiple_of(128 * t, 128), 128)]
        dst = relay.at[pl.ds(3 * me, 3)]

        @pl.when(to != me)
        def _():
            remote(src, dst, h1_send, h1_recv, to).start()

        @pl.when(to == me)
        def _():
            pltpu.make_async_copy(src, dst, h1_recv).start()

        return carry

    lax.fori_loop(0, 2 * CORES_TILES, to_relay, 0)

    columns[0] = fresh_ref[:, :, mine_lanes]
    swap.wait_recv()
    both = align_layer(columns[...].reshape(336, RP), core)
    high, low = split(both)
    gram[...] = lax.dot_general(
        jnp.concatenate([high, high, low], axis=0),
        jnp.concatenate([high, low, high], axis=0),
        (((0,), (0,)), ((), ())),
        preferred_element_type=F32,
    )
    pack(gram, packed)

    def share(c):
        return pl.ds(pl.multiple_of(24 * c, 8), 24)

    def reduce_push(i, carry):
        to = jnp.bitwise_xor(chip, i)
        remote(packed.at[share(to)], terms.at[chip], rs_send, rs_recv, to * 2 + core).start()
        return carry

    lax.fori_loop(1, CHIPS, reduce_push, 0)
    terms[pl.ds(chip, 1)] = packed[share(chip)][None]
    drain(terms.at[pl.ds(0, CHIPS - 1)], rs_recv)
    summed[share(chip)] = jnp.sum(terms[...], axis=0)

    def gather_push(i, carry):
        to = jnp.bitwise_xor(chip, i)
        part = summed.at[share(chip)]
        remote(part, part, ag_send, ag_recv, to * 2 + core).start()
        return carry

    lax.fori_loop(1, CHIPS, gather_push, 0)

    layer = 1 - core
    u = jnp.where(layer == 0, chip, 63 - chip)
    lane_tile = u // 7
    q = lax.rem(u, 7)

    @pl.when(u < CORES_TILES)
    def _():
        drain(relay, h1_recv)

        def choose(b, carry):
            chosen[pl.ds(b, 1)] = relay[pl.ds(slot_ref[b], 1)]
            return carry

        lax.fori_loop(0, DEVICES, choose, 0)

        def to_columns(b, carry):
            octet = 7 * b + q
            to = (octet // 16) * 2 + layer
            dst = mcol.at[
                pl.ds(pl.multiple_of(8 * lax.rem(octet, 16), 8), 8),
                pl.ds(pl.multiple_of(128 * lane_tile, 128), 128),
            ]
            remote(chosen.at[b], dst, h2_send, h2_recv, to).start()
            return carry

        lax.fori_loop(0, DEVICES, to_columns, 0)

    drain(summed.at[pl.ds(0, 24 * (CHIPS - 1))], ag_recv)
    unpack(summed, gram)

    diag = lax.broadcasted_iota(jnp.int32, (RP, RP), 0) == lax.broadcasted_iota(jnp.int32, (RP, RP), 1)
    squares = jnp.sum(jnp.where(diag, gram[...], 0.0), axis=(0, 1), keepdims=True)
    inverse = 1.0 / (jnp.sqrt(squares) + epsilon)
    gram[...] = gram[...] * (inverse * inverse)

    @pl.when(chip < 56)
    def _():
        drain(mcol, h2_recv)

    @pl.when(chip >= 56)
    def _():
        mcol[...] = jnp.zeros_like(mcol)

    left_form(align_layer(mcol[...], core) * inverse, xa)

    def polynomial():
        g = gram[...]
        left_form(g, ga)
        right_form(g, gb)
        p = coef_b * g + coef_c * dot(ga[...], gb[...])
        right_form(jnp.where(diag, p + coef_a, p), pb)

    def sweep(i, carry):
        polynomial()
        left_form(dot(xa[...], pb[...]), xa)
        left_form(dot(ga[...], pb[...]), ta)
        gram[...] = dot(ta[...], pb[...])
        return carry

    lax.fori_loop(0, ITERS - 1, sweep, 0)
    polynomial()
    result = dot(xa[...], pb[...]) * (0.2 * math.sqrt(max(R, 7168)))
    tile_ref[...] = result.T[0:R, :].astype(BF16)

    swap.wait_send()
    drain(terms.at[pl.ds(0, CHIPS - 1)], rs_send)
    drain(summed.at[pl.ds(0, 24 * (CHIPS - 1))], ag_send)

    @pl.when(u < CORES_TILES)
    def _():
        drain(relay.at[pl.ds(0, 3 * (2 * CORES_TILES - 1))], h1_send)
        drain(chosen, h2_send)

    @pl.when(u >= CORES_TILES)
    def _():
        drain(relay.at[pl.ds(0, 3 * 2 * CORES_TILES)], h1_send)


def iterate(fresh, slot_index):
    return pl.pallas_call(
        iterate_kernel,
        out_shape=jax.ShapeDtypeStruct((R, 128), BF16),
        in_specs=[
            pl.BlockSpec(memory_space=pltpu.VMEM),
            pl.BlockSpec(memory_space=pltpu.SMEM),
        ],
        out_specs=pl.BlockSpec(memory_space=pltpu.VMEM),
        scratch_shapes=[
            pltpu.VMEM((2, 3, 56, RP), F32),
            pltpu.VMEM((1536, 128), F32),
            pltpu.VMEM((CHIPS, 24, 128), F32),
            pltpu.VMEM((1536, 128), F32),
            pltpu.VMEM((384, 8, 128), F32),
            pltpu.VMEM((DEVICES, 8, 128), F32),
            pltpu.VMEM((128, RP), F32),
            pltpu.VMEM((RP, RP), F32),
            pltpu.VMEM((RP, 3 * RP), BF16),
            pltpu.VMEM((3 * RP, RP), BF16),
            pltpu.VMEM((3 * RP, RP), BF16),
            pltpu.VMEM((RP, 3 * RP), BF16),
            pltpu.VMEM((128, 3 * RP), BF16),
        ]
        + [pltpu.SemaphoreType.DMA] * 10,
        compiler_params=pltpu.CompilerParams(
            collective_id=1, has_side_effects=True, vmem_limit_bytes=50 * 2**20
        ),
        name="iterate",
    )(fresh, slot_index)


ORDERS = ("xyz", "yzx", "zxy")


def gather_kernel(tile_ref, out, local_sem, send, recv, sib_send, sib_recv):
    me, chip, core = position()
    home = {"y": chip // 16, "z": lax.rem(chip // 4, 4), "x": lax.rem(chip, 4)}
    sibling = chip * 2 + 1 - core

    def shift(axis, step):
        moved = dict(home)
        moved[axis] = lax.rem(home[axis] + step + 4, 4)
        return moved

    def device(at):
        return ((at["y"] * 4 + at["z"]) * 4 + at["x"]) * 2 + core

    barrier = pltpu.get_barrier_semaphore()
    for other in [device(shift(axis, step)) for axis in "yzx" for step in (1, -1)] + [sibling]:
        pl.semaphore_signal(barrier, inc=1, device_id=(other,), device_id_type=MESH)
    pl.semaphore_wait(barrier, 7)

    def held(part, phase, at):
        y, z, x = at["y"], at["z"], at["x"]
        if phase == 0:
            return [(128 * (16 * y + 4 * z + x), 128)]
        if part == 0:
            if phase == 1:
                return [(512 * (4 * y + z), 512)]
            return [(512 * (4 * s + z), 512) for s in range(4)]
        if part == 1:
            if phase == 1:
                return [(128 * (16 * s + 4 * z + x), 128) for s in range(4)]
            return [(128 * (16 * s + 4 * t + x), 128) for s in range(4) for t in range(4)]
        if phase == 1:
            return [(128 * (16 * y + 4 * s + x), 128) for s in range(4)]
        return [(2048 * y, 2048)]

    def view(part, columns, half):
        row = R * core + 192 * part + (0 if half is None else 96 * half)
        return out.at[
            pl.ds(pl.multiple_of(row, 16), 192 if half is None else 96),
            pl.ds(pl.multiple_of(columns[0], 128), columns[1]),
        ]

    def push(part, columns, send_sem, recv_sem, to, half=None):
        for item in columns:
            block = view(part, item, half)
            remote(block, block, send_sem, recv_sem, to).start()

    def drain_size(sem, rows, width):
        drain(out.at[pl.ds(0, rows), pl.ds(0, width)], sem)

    own = pltpu.make_async_copy(
        tile_ref,
        out.at[pl.ds(pl.multiple_of(R * core, 16), R), pl.ds(pl.multiple_of(128 * chip, 128), 128)],
        local_sem,
    )
    own.start()
    own.wait()
    sides = ((0, 1), (1, -1))
    for phase in range(3):
        width = 128 * 4**phase
        for part in range(3):
            axis = ORDERS[part][phase]
            for d, step in sides:
                push(part, held(part, phase, home), send.at[part, phase, 0, d], recv.at[part, phase, 0, d], device(shift(axis, step)))
        if phase == 2:
            for part in range(3):
                push(part, held(part, 2, home), sib_send.at[part], sib_recv.at[part], sibling)
        for part in range(3):
            axis = ORDERS[part][phase]
            for d, step in sides:
                drain_size(recv.at[part, phase, 0, d], 192, width)
                arrived = held(part, phase, shift(axis, -step))
                push(part, arrived, send.at[part, phase, 1, d], recv.at[part, phase, 1, d], device(shift(axis, step)), half=d)
                if phase == 2:
                    n = 3 + 2 * part + d
                    push(part, arrived, sib_send.at[n], sib_recv.at[n], sibling)
        for part in range(3):
            axis = ORDERS[part][phase]
            for d, step in sides:
                drain_size(recv.at[part, phase, 1, d], 96, width)
                if phase == 2:
                    n = 9 + 2 * part + d
                    push(part, held(part, phase, shift(axis, -2 * step)), sib_send.at[n], sib_recv.at[n], sibling, half=d)
    for part in range(3):
        for phase in range(3):
            for d in range(2):
                drain_size(send.at[part, phase, 0, d], 192, 128 * 4**phase)
                drain_size(send.at[part, phase, 1, d], 96, 128 * 4**phase)
    for n in range(15):
        drain_size(sib_send.at[n], 192 if n < 9 else 96, 2048)
        drain_size(sib_recv.at[n], 192 if n < 9 else 96, 2048)


def gather(tile):
    return pl.pallas_call(
        gather_kernel,
        out_shape=jax.ShapeDtypeStruct((2 * R, 128 * CHIPS), BF16),
        in_specs=[pl.BlockSpec(memory_space=pltpu.VMEM)],
        out_specs=pl.BlockSpec(memory_space=pl.ANY),
        scratch_shapes=[
            pltpu.SemaphoreType.DMA,
            pltpu.SemaphoreType.DMA((3, 3, 2, 2)),
            pltpu.SemaphoreType.DMA((3, 3, 2, 2)),
            pltpu.SemaphoreType.DMA((15,)),
            pltpu.SemaphoreType.DMA((15,)),
        ],
        compiler_params=pltpu.CompilerParams(
            collective_id=2, has_side_effects=True, vmem_limit_bytes=50 * 2**20
        ),
        name="gather",
    )(tile)


def slot_of_blocks(table, slot_count):
    positions = jnp.arange(table.shape[0], dtype=jnp.int32)
    matching = (table[None, :] == table[:, None]) & (positions[None, :] < positions[:, None])
    ranking = jnp.sum(matching.astype(jnp.int32), axis=1)
    return table * slot_count + ranking


def local(grads, momentum, table):
    me = lax.axis_index("dp")
    slot_index = slot_of_blocks(table, 3)
    hits = slot_index[None, :] == jnp.arange(384, dtype=jnp.int32)[:, None]
    count = jnp.sum((table == me).astype(jnp.int32))
    mine = (jnp.arange(3, dtype=jnp.int32) < count).astype(F32)
    pieces = jnp.pad(grads.reshape(9, 128, 56), ((0, 1), (0, 0), (0, 8)))
    pieces = pieces.transpose(1, 0, 2).reshape(128, 640)
    outgoing = jnp.dot(hits.astype(BF16), pieces, preferred_element_type=F32).astype(BF16)
    outgoing = jnp.pad(outgoing.reshape(128, 15, 128), ((0, 0), (0, 1), (0, 0)))
    fresh = scatter(outgoing, momentum, mine)
    tile = iterate(fresh, slot_index)
    update = gather(tile)[:, :7168]
    return update, fresh


def solution(mesh):
    in_specs = (P("dp", None), P("dp", None, None), P())
    out_specs = (P(), P("dp", None, None))
    return jax.shard_map(local, mesh=mesh, in_specs=in_specs, out_specs=out_specs, check_vma=False)
```

```python
import math

import jax
import jax.numpy as jnp
from jax import lax
from jax.experimental import pallas as pl
from jax.experimental.pallas import tpu as pltpu
from jax.sharding import PartitionSpec as P

R = 576
ITERS = 5
RP = 640
K3 = 1792
DEVICES = 128
CHIPS = 64
TILES = 56
RELAYS = 35
MESH = pl.DeviceIdType.MESH
F32 = jnp.float32
BF16 = jnp.bfloat16

coef_a = 3.4445
coef_b = -4.775
coef_c = 2.0315
epsilon = 1e-07


def position():
    me = lax.axis_index("dp")
    return me, me // 2, lax.rem(me, 2)


def remote(src, dst, send, recv, to):
    return pltpu.make_async_remote_copy(
        src, dst, send, recv, device_id=(to,), device_id_type=MESH
    )


def drain(view, sem):
    pltpu.make_async_copy(view, view, sem).wait()


def split(value):
    high = value.astype(BF16)
    return high, (value - high.astype(F32)).astype(BF16)


def dot(a, b):
    return jnp.dot(a, b, preferred_element_type=F32)


def window_start(t):
    return min(128 * t // 9, DEVICES - 16)


def align_layer(value, core):
    moved = pltpu.roll(value, (RP - 64) * core, 1)
    lane = lax.broadcasted_iota(jnp.int32, value.shape, 1)
    return jnp.where(lane < R, moved, 0.0)


STRIP = (0, 576, 1024, 1344)


def pack(gram, packed):
    lane = lax.broadcasted_iota(jnp.int32, (64, 128), 1)
    corner = pltpu.roll(gram[512:576, 512:640], 64, 1)
    packed[0:64, :] = jnp.where(lane < 64, gram[0:64, 0:128], corner)
    packed[64:576, :] = gram[64:576, 0:128]
    for s in range(1, 4):
        packed[STRIP[s] : STRIP[s] + 576 - 128 * s, :] = gram[
            128 * s : 576, 128 * s : 128 * s + 128
        ]


def unpack(packed, gram):
    row = lax.broadcasted_iota(jnp.int32, (128, 128), 0)
    lane = lax.broadcasted_iota(jnp.int32, (128, 128), 1)
    upper = (row < 64) & (lane >= 64)
    first = packed[0:128, :]
    clean = jnp.where(upper, 0.0, first)
    gram[0:128, 0:128] = jnp.where(upper, clean.T, clean)
    corner = pltpu.roll(packed[0:64, :], 64, 1)
    lane64 = lax.broadcasted_iota(jnp.int32, (64, 128), 1)
    gram[512:576, 512:640] = jnp.where(lane64 < 64, corner, 0.0)
    for s in range(4):
        for b in range(s, 5):
            if b == s:
                if s:
                    gram[128 * s : 128 * s + 128, 128 * s : 128 * s + 128] = packed[
                        STRIP[s] : STRIP[s] + 128, :
                    ]
                continue
            n = 64 if b == 4 else 128
            start = STRIP[s] + 128 * (b - s)
            block = packed[start : start + n, :]
            gram[128 * b : 128 * b + n, 128 * s : 128 * s + 128] = block
            if n == 64:
                block = jnp.concatenate([block, jnp.zeros((64, 128), F32)], axis=0)
            gram[128 * s : 128 * s + 128, 128 * b : 128 * b + 128] = block.T


def greet_all(me, ready):
    barrier = pltpu.get_barrier_semaphore()
    for i in [*range(1, 16), *range(16, DEVICES, 16)]:
        pl.semaphore_signal(
            barrier, inc=1, device_id=(jnp.bitwise_xor(me, i),), device_id_type=MESH
        )

    def finish():
        pl.semaphore_wait(barrier, 22)
        for i in range(16, DEVICES, 16):
            pl.semaphore_signal(
                ready, inc=1, device_id=(jnp.bitwise_xor(me, i),), device_id_type=MESH
            )
        pl.semaphore_wait(ready, 7)

    return finish


def left_form(value, ref):
    high, low = split(value)
    tail = value[:, 512:RP]
    ref[:, 0:512] = high[:, 0:512]
    ref[:, 512:1024] = high[:, 0:512]
    ref[:, 1024:1536] = low[:, 0:512]
    ref[:, 1536:1664] = (tail + pltpu.roll(tail, 64, 1)).astype(BF16)
    ref[:, 1664:1792] = low[:, 512:RP]


def right_form(value, ref):
    high, low = split(value)
    ref[0:512, :] = high[0:512]
    ref[512:1024, :] = low[0:512]
    ref[1024:1536, :] = high[0:512]
    ref[1536:1600, :] = high[512:R]
    ref[1600:1664, :] = low[512:R]
    ref[1664:1728, :] = high[512:R]


def symmetric_dot(left, right, out):
    c0 = dot(left[...], right[:, 0:256])
    c1 = dot(left[256:R, :], right[:, 256:512])
    c2 = dot(left[512:R, :], right[:, 512:RP])
    blank = jnp.zeros((64, 256), F32)
    out[:, 0:256] = c0
    out[256:R, 256:512] = c1
    out[512:R, 512:RP] = c2
    out[0:256, 256:512] = c0[256:512].T
    out[0:256, 512:RP] = jnp.concatenate([c0[512:R], blank], axis=0).T
    out[256:512, 512:RP] = jnp.concatenate([c1[256:320], blank], axis=0).T


ORDERS = ("xyz", "yzx", "zxy")
OFFSETS = (0, -1, 1, 2)
SIDES = ((0, 1), (1, -1))


def gather_steps(buf, send, recv, sib_send, sib_recv):
    me, chip, core = position()
    home = {"y": chip // 16, "z": lax.rem(chip // 4, 4), "x": lax.rem(chip, 4)}
    sibling = chip * 2 + 1 - core
    parts = range(3)

    def shift(at, axis, step):
        moved = dict(at)
        moved[axis] = lax.rem(at[axis] + step + 4, 4)
        return moved

    def device(at):
        return ((at["y"] * 4 + at["z"]) * 4 + at["x"]) * 2 + core

    def rows_of(part, half):
        row = R * core + 192 * part + (0 if half is None else 96 * half)
        return pl.ds(pl.multiple_of(row, 16), 192 if half is None else 96)

    def line(part, at):
        y, z, x = at["y"], at["z"], at["x"]
        if part == 0:
            return jnp.logical_or(y < 3, z < 2), 4, 0, lambda n: (y, z, pl.ds(0, n))
        if part == 1:
            return z < 2, 4, 3, lambda n: (pl.ds(0, n), z, x)
        return y < 3, 4, 2, lambda n: (y, pl.ds(0, n), x)

    def tile(part, at):
        y, z, x = at["y"], at["z"], at["x"]
        return jnp.logical_or(y < 3, z < 2), 1, 0, lambda n: (y, z, pl.ds(x, n))

    def each(spec, act):
        whole, count, fewer, index = spec

        @pl.when(whole)
        def _():
            act(count, index(count))

        if fewer:

            @pl.when(jnp.logical_not(whole))
            def _():
                act(fewer, index(fewer))

    def push(part, spec, send_sem, recv_sem, to, half=None):
        def act(count, index):
            block = buf.at[(*index, rows_of(part, half))]
            remote(block, block, send_sem, recv_sem, to).start()

        each(spec, act)

    def take(spec, sem, half=None):
        def act(count, index):
            drain(buf.at[0, 0, pl.ds(0, count), pl.ds(0, 192 if half is None else 96)], sem)

        each(spec, act)

    def both(part, k, spec, axis):
        for d, step in SIDES:
            push(part, spec, send.at[part, k, d], recv.at[part, k, d], device(shift(home, axis, step)))

    def pass_on(part, k, spec, d, axis, step):
        push(part, spec, send.at[part, k, d], recv.at[part, k, d], device(shift(home, axis, step)), half=d)

    def tell(part, n, spec, half=None):
        push(part, spec, sib_send.at[part, n], sib_recv.at[part, n], sibling, half=half)

    def near(part, axis, step, i):
        return line(part, shift(shift(home, axis, step), ORDERS[part][1], OFFSETS[i]))

    def forward(part, i):
        axis = ORDERS[part][2]
        for d, step in SIDES:
            got = near(part, axis, -step, i)
            take(got, recv.at[part, 4 + i, d])
            pass_on(part, 8 + i, got, d, axis, step)
            tell(part, 4 + 2 * i + d, got)

    for p in parts:
        both(p, 0, tile(p, home), ORDERS[p][0])
    for p in parts:
        axis = ORDERS[p][0]
        for d, step in SIDES:
            got = tile(p, shift(home, axis, -step))
            take(got, recv.at[p, 0, d])
            pass_on(p, 1, got, d, axis, step)
    for p in parts:
        first, second, third = ORDERS[p]
        for d, step in SIDES:
            take(tile(p, shift(home, first, 2)), recv.at[p, 1, d], half=d)
        both(p, 2, line(p, home), second)
        both(p, 4, line(p, home), third)
        tell(p, 0, line(p, home))
    for p in parts:
        _, second, third = ORDERS[p]
        for d, step in SIDES:
            got = line(p, shift(home, second, -step))
            take(got, recv.at[p, 2, d])
            pass_on(p, 3, got, d, second, step)
            both(p, 5 + d, got, third)
            tell(p, 1 + d, got)
    for p in parts:
        forward(p, 0)
    for p in parts:
        _, second, third = ORDERS[p]
        got = line(p, shift(home, second, 2))
        for d, step in SIDES:
            take(got, recv.at[p, 3, d], half=d)
        both(p, 7, got, third)
        tell(p, 3, got)
    for i in (1, 2, 3):
        for p in parts:
            forward(p, i)
    for i in range(4):
        for p in parts:
            got = near(p, ORDERS[p][2], 2, i)
            for d, step in SIDES:
                take(got, recv.at[p, 8 + i, d], half=d)
                tell(p, 12 + 2 * i + d, got, half=d)

    for p in parts:
        first, second, third = ORDERS[p]
        for d, step in SIDES:
            take(tile(p, home), send.at[p, 0, d])
            take(tile(p, shift(home, first, -step)), send.at[p, 1, d], half=d)
            take(line(p, home), send.at[p, 2, d])
            take(line(p, shift(home, second, -step)), send.at[p, 3, d], half=d)
            for i in range(4):
                take(near(p, third, 0, i), send.at[p, 4 + i, d])
                take(near(p, third, -step, i), send.at[p, 8 + i, d], half=d)
        for sem in (sib_send, sib_recv):
            for i in range(4):
                take(near(p, third, 0, i), sem.at[p, i])
                for d, step in SIDES:
                    take(near(p, third, -step, i), sem.at[p, 4 + 2 * i + d])
                    take(near(p, third, 2, i), sem.at[p, 12 + 2 * i + d], half=d)


def step_kernel(
    out_ref, mom_ref, mine_ref, slot_ref, fresh_ref, buf,
    got, place, columns, packed, terms, summed, relay, chosen, arrived, mcol,
    gram, gram2, ga, gb, pbs, ta, xa, ready,
    a2a_send, a2a_recv, swap_send, swap_recv, rs_send, rs_recv, ag_send, ag_recv,
    h1_send, h1_recv, h2_send, h2_recv, send, recv, sib_send, sib_recv,
):
    me, chip, core = position()
    greeted = greet_all(me, ready)

    rows = lax.broadcasted_iota(jnp.int32, (256, 128), 0)
    lanes = lax.broadcasted_iota(jnp.int32, (1, 128), 1)
    for t in range(9):
        row = lanes + 128 * t
        source = lax.shift_right_logical(row * 7282, 16)
        r = row - 9 * source
        half = lax.shift_right_logical(r, 1)
        odd = r - 2 * half
        base = 16 * (source - window_start(t)) + half
        for k in range(3):
            for parity in range(2):
                target = jnp.where(odd == parity, base + 5 * k, -1)
                place[t, :, pl.ds(128 * (2 * k + parity), 128)] = jnp.where(
                    rows == target, 1.0, 0.0
                ).astype(BF16)
    greeted()

    def push(i, carry):
        to = jnp.bitwise_xor(me, i)
        remote(out_ref.at[to], got.at[me], a2a_send, a2a_recv, to).start()
        return carry

    lax.fori_loop(1, DEVICES, push, 0)
    got[pl.ds(me, 1)] = out_ref[pl.ds(me, 1)]
    for i in range(ITERS):
        pbs[i, 1728:K3, :] = jnp.zeros((K3 - 1728, RP), BF16)
    gb[1728:K3, :] = jnp.zeros((K3 - 1728, RP), BF16)
    chosen[DEVICES : DEVICES + 2] = jnp.zeros((2, 8, 128), F32)
    others = got.at[pl.ds(0, DEVICES - 1)]
    drain(others, a2a_recv)
    for t in range(9):
        window = got[pl.ds(window_start(t), 16)].reshape(256, 128)
        placed = lax.dot_general(
            window, place[t], (((0,), (0,)), ((), ())), preferred_element_type=F32
        )
        for k in range(3):
            grad = (
                placed[0:56, 256 * k : 256 * k + 128]
                + placed[64:120, 256 * k + 128 : 256 * k + 256]
            )
            fresh_ref[k, :, pl.ds(128 * t, 128)] = (
                0.95 * mom_ref[k, :, pl.ds(128 * t, 128)] + grad
            ) * mine_ref[k]

    sibling = chip * 2 + 1 - core
    mine_lanes = pl.ds(pl.multiple_of(512 * core, 128), RP)
    their_lanes = pl.ds(pl.multiple_of(512 * (1 - core), 128), RP)
    swap = remote(fresh_ref.at[:, :, their_lanes], columns.at[1], swap_send, swap_recv, sibling)
    swap.start()
    columns[0] = fresh_ref[:, :, mine_lanes]
    swap.wait_recv()
    both = align_layer(columns[...].reshape(336, RP), core)
    high, low = split(both)
    gram[...] = lax.dot_general(
        jnp.concatenate([high, high, low], axis=0),
        jnp.concatenate([high, low, high], axis=0),
        (((0,), (0,)), ((), ())),
        preferred_element_type=F32,
    )[0:R]
    pack(gram, packed)

    def share(c):
        return pl.ds(pl.multiple_of(24 * c, 8), 24)

    def reduce_push(i, carry):
        to = jnp.bitwise_xor(chip, i)
        remote(packed.at[share(to)], terms.at[chip], rs_send, rs_recv, to * 2 + core).start()
        return carry

    lax.fori_loop(1, CHIPS, reduce_push, 0)
    terms[pl.ds(chip, 1)] = packed[share(chip)][None]
    drain(terms.at[pl.ds(0, CHIPS - 1)], rs_recv)
    summed[share(chip)] = jnp.sum(terms[...], axis=0)

    def gather_push(i, carry):
        to = jnp.bitwise_xor(chip, i)
        part = summed.at[share(chip)]
        remote(part, part, ag_send, ag_recv, to * 2 + core).start()
        return carry

    lax.fori_loop(1, CHIPS, gather_push, 0)

    def to_relay(i, carry):
        layer = i // RELAYS
        u = lax.rem(i, RELAYS)
        t = u // 7 + 4 * layer
        q = lax.rem(u, 7)
        to = jnp.where(layer == 0, u * 2 + 1, (63 - u) * 2)
        src = fresh_ref.at[
            :, pl.ds(pl.multiple_of(8 * q, 8), 8), pl.ds(pl.multiple_of(128 * t, 128), 128)
        ]
        dst = relay.at[pl.ds(3 * me, 3)]

        @pl.when(to != me)
        def _():
            remote(src, dst, h1_send, h1_recv, to).start()

        @pl.when(to == me)
        def _():
            pltpu.make_async_copy(src, dst, h1_recv).start()

        return carry

    lax.fori_loop(0, 2 * RELAYS, to_relay, 0)

    drain(summed.at[pl.ds(0, 24 * (CHIPS - 1))], ag_recv)
    unpack(summed, gram)
    diag = lax.broadcasted_iota(jnp.int32, (R, RP), 0) == lax.broadcasted_iota(jnp.int32, (R, RP), 1)
    squares = jnp.sum(jnp.where(diag, gram[...], 0.0), axis=(0, 1), keepdims=True)
    inverse = 1.0 / (jnp.sqrt(squares) + epsilon)
    gram[...] = gram[...] * (inverse * inverse)

    def polynomial(i):
        g = gram[...]
        left_form(g, ga)
        right_form(g, gb)
        symmetric_dot(ga, gb, gram2)
        p = coef_b * g + coef_c * gram2[...]
        right_form(jnp.where(diag, p + coef_a, p), pbs.at[i])

    def sweep(i, carry):
        polynomial(i)
        symmetric_dot(ga, pbs.at[i], gram2)
        left_form(gram2[...], ta)
        symmetric_dot(ta, pbs.at[i], gram)
        return carry

    lax.fori_loop(0, 2, sweep, 0)

    layer = 1 - core
    u = jnp.where(layer == 0, chip, 63 - chip)
    lane_tile = u // 7
    q = lax.rem(u, 7)

    def first_block(j, q):
        return (16 * j - q + 6) // 7

    @pl.when(u < RELAYS)
    def _():
        drain(relay, h1_recv)

        def choose(b, carry):
            chosen[pl.ds(b, 1)] = relay[pl.ds(slot_ref[b], 1)]
            return carry

        lax.fori_loop(0, DEVICES, choose, 0, unroll=8)

        def to_columns(j, carry):
            src = chosen.at[pl.ds(first_block(j, q), 3)]
            remote(src, arrived.at[lane_tile, q], h2_send, h2_recv, j * 2 + layer).start()
            return carry

        lax.fori_loop(0, TILES, to_columns, 0)

    lax.fori_loop(2, ITERS - 1, sweep, 0)
    polynomial(ITERS - 1)

    @pl.when(chip < TILES)
    def _():
        drain(arrived, h2_recv)
        for i in range(16):
            octet = 16 * chip + i
            block = octet // 7
            r = octet - 7 * block
            for t in range(5):
                mcol[8 * i : 8 * i + 8, 128 * t : 128 * t + 128] = arrived[
                    t, r, block - first_block(chip, r)
                ]

    @pl.when(chip >= TILES)
    def _():
        mcol[...] = jnp.zeros_like(mcol)

    value = align_layer(mcol[...], core) * inverse

    def apply(i, value):
        left_form(value, xa)
        return dot(xa[...], pbs[i])

    value = lax.fori_loop(0, ITERS, apply, value) * (0.2 * math.sqrt(max(R, 7168)))
    buf[chip // 16, lax.rem(chip // 4, 4), lax.rem(chip, 4), pl.ds(pl.multiple_of(R * core, 16), R)] = (
        value.T[0:R, :].astype(BF16)
    )
    gather_steps(buf, send, recv, sib_send, sib_recv)

    drain(others, a2a_send)
    swap.wait_send()
    drain(terms.at[pl.ds(0, CHIPS - 1)], rs_send)
    drain(summed.at[pl.ds(0, 24 * (CHIPS - 1))], ag_send)

    @pl.when(u < RELAYS)
    def _():
        drain(relay.at[pl.ds(0, 3 * (2 * RELAYS - 1))], h1_send)
        drain(relay.at[pl.ds(0, 3 * TILES)], h2_send)

    @pl.when(u >= RELAYS)
    def _():
        drain(relay.at[pl.ds(0, 3 * 2 * RELAYS)], h1_send)


def step(outgoing, momentum, mine, slot_index):
    return pl.pallas_call(
        step_kernel,
        out_shape=(
            jax.ShapeDtypeStruct(momentum.shape, F32),
            pltpu.VMEM((4, 4, 4, 2 * R, 128), BF16),
        ),
        in_specs=[
            pl.BlockSpec(memory_space=pltpu.VMEM),
            pl.BlockSpec(memory_space=pltpu.VMEM),
            pl.BlockSpec(memory_space=pltpu.SMEM),
            pl.BlockSpec(memory_space=pltpu.SMEM),
        ],
        out_specs=(
            pl.BlockSpec(memory_space=pltpu.VMEM),
            pl.BlockSpec(memory_space=pltpu.VMEM),
        ),
        scratch_shapes=[
            pltpu.VMEM((DEVICES, 16, 128), BF16),
            pltpu.VMEM((9, 256, 768), BF16),
            pltpu.VMEM((2, 3, 56, RP), F32),
            pltpu.VMEM((1536, 128), F32),
            pltpu.VMEM((CHIPS, 24, 128), F32),
            pltpu.VMEM((1536, 128), F32),
            pltpu.VMEM((384, 8, 128), F32),
            pltpu.VMEM((DEVICES + 2, 8, 128), F32),
            pltpu.VMEM((5, 7, 3, 8, 128), F32),
            pltpu.VMEM((128, RP), F32),
            pltpu.VMEM((R, RP), F32),
            pltpu.VMEM((R, RP), F32),
            pltpu.VMEM((R, K3), BF16),
            pltpu.VMEM((K3, RP), BF16),
            pltpu.VMEM((ITERS, K3, RP), BF16),
            pltpu.VMEM((R, K3), BF16),
            pltpu.VMEM((128, K3), BF16),
            pltpu.SemaphoreType.REGULAR,
        ]
        + [pltpu.SemaphoreType.DMA] * 12
        + [pltpu.SemaphoreType.DMA((3, 12, 2))] * 2
        + [pltpu.SemaphoreType.DMA((3, 20))] * 2,
        compiler_params=pltpu.CompilerParams(
            collective_id=0, has_side_effects=True, vmem_limit_bytes=40 * 2**20
        ),
        name="step",
    )(outgoing, momentum, mine, slot_index)


def place_kernel(buf, update, sem):
    copies = [
        pltpu.make_async_copy(
            buf.at[j // 16, j // 4 % 4, j % 4], update.at[:, pl.ds(128 * j, 128)], sem.at[j]
        )
        for j in range(TILES)
    ]
    for copy in copies:
        copy.start()
    for copy in copies:
        copy.wait()


def place_tiles(buf):
    return pl.pallas_call(
        place_kernel,
        out_shape=jax.ShapeDtypeStruct((2 * R, 128 * TILES), BF16),
        in_specs=[pl.BlockSpec(memory_space=pl.ANY)],
        out_specs=pl.BlockSpec(memory_space=pl.ANY),
        scratch_shapes=[pltpu.SemaphoreType.DMA((TILES,))],
        compiler_params=pltpu.CompilerParams(vmem_limit_bytes=2 * 2**20),
        name="place",
    )(buf)


def slot_of_blocks(table, slot_count):
    positions = jnp.arange(table.shape[0], dtype=jnp.int32)
    matching = (table[None, :] == table[:, None]) & (positions[None, :] < positions[:, None])
    ranking = jnp.sum(matching.astype(jnp.int32), axis=1)
    return table * slot_count + ranking


def local(grads, momentum, table):
    me = lax.axis_index("dp")
    slot_index = slot_of_blocks(table, 3)
    hits = slot_index[None, :] == jnp.arange(384, dtype=jnp.int32)[:, None]
    count = jnp.sum((table == me).astype(jnp.int32))
    mine = (jnp.arange(3, dtype=jnp.int32) < count).astype(F32)
    pieces = jnp.pad(grads.reshape(9, 128, 56), ((0, 1), (0, 0), (0, 8)))
    pieces = pieces.transpose(1, 0, 2).reshape(128, 640)
    outgoing = jnp.dot(hits.astype(BF16), pieces, preferred_element_type=F32).astype(BF16)
    outgoing = jnp.pad(outgoing.reshape(128, 15, 128), ((0, 0), (0, 1), (0, 0)))
    fresh, buf = step(outgoing, momentum, mine, slot_index)
    return place_tiles(buf), fresh


def solution(mesh):
    in_specs = (P("dp", None), P("dp", None, None), P())
    out_specs = (P(), P("dp", None, None))
    return jax.shard_map(local, mesh=mesh, in_specs=in_specs, out_specs=out_specs, check_vma=False)
```

```python
import math

import jax
import jax.numpy as jnp
from jax import lax
from jax.experimental import pallas as pl
from jax.experimental.pallas import tpu as pltpu
from jax.sharding import PartitionSpec as P

R = 576
ITERS = 5
RP = 640
K3 = 1792
DEVICES = 128
CHIPS = 64
TILES = 56
RELAYS = 63
MESH = pl.DeviceIdType.MESH
F32 = jnp.float32
BF16 = jnp.bfloat16

coef_a = 3.4445
coef_b = -4.775
coef_c = 2.0315
epsilon = 1e-07


def position():
    me = lax.axis_index("dp")
    return me, me // 2, lax.rem(me, 2)


def remote(src, dst, send, recv, to):
    return pltpu.make_async_remote_copy(
        src, dst, send, recv, device_id=(to,), device_id_type=MESH
    )


def drain(view, sem):
    pltpu.make_async_copy(view, view, sem).wait()


def split(value):
    high = value.astype(BF16)
    return high, (value - high.astype(F32)).astype(BF16)


def dot(a, b):
    return jnp.dot(a, b, preferred_element_type=F32)


def window_start(t):
    return min(128 * t // 9, DEVICES - 16)


def align_layer(value, core):
    moved = pltpu.roll(value, (RP - 64) * core, 1)
    lane = lax.broadcasted_iota(jnp.int32, value.shape, 1)
    return jnp.where(lane < R, moved, 0.0)


STRIP = (0, 576, 1024, 1344)


def pack(gram, packed):
    lane = lax.broadcasted_iota(jnp.int32, (64, 128), 1)
    corner = pltpu.roll(gram[512:576, 512:640], 64, 1)
    packed[0:64, :] = jnp.where(lane < 64, gram[0:64, 0:128], corner)
    packed[64:576, :] = gram[64:576, 0:128]
    for s in range(1, 4):
        packed[STRIP[s] : STRIP[s] + 576 - 128 * s, :] = gram[
            128 * s : 576, 128 * s : 128 * s + 128
        ]


def unpack(packed, gram):
    row = lax.broadcasted_iota(jnp.int32, (128, 128), 0)
    lane = lax.broadcasted_iota(jnp.int32, (128, 128), 1)
    upper = (row < 64) & (lane >= 64)
    first = packed[0:128, :]
    clean = jnp.where(upper, 0.0, first)
    gram[0:128, 0:128] = jnp.where(upper, clean.T, clean)
    corner = pltpu.roll(packed[0:64, :], 64, 1)
    lane64 = lax.broadcasted_iota(jnp.int32, (64, 128), 1)
    gram[512:576, 512:640] = jnp.where(lane64 < 64, corner, 0.0)
    for s in range(4):
        for b in range(s, 5):
            if b == s:
                if s:
                    gram[128 * s : 128 * s + 128, 128 * s : 128 * s + 128] = packed[
                        STRIP[s] : STRIP[s] + 128, :
                    ]
                continue
            n = 64 if b == 4 else 128
            start = STRIP[s] + 128 * (b - s)
            block = packed[start : start + n, :]
            gram[128 * b : 128 * b + n, 128 * s : 128 * s + 128] = block
            if n == 64:
                block = jnp.concatenate([block, jnp.zeros((64, 128), F32)], axis=0)
            gram[128 * s : 128 * s + 128, 128 * b : 128 * b + 128] = block.T


def spread(count, factor, act):
    for i in range(1, 8):
        act((i * factor) % count)

    def block(b, carry):
        for i in range(8):
            act(jnp.bitwise_and((8 * b + i) * factor, count - 1))
        return carry

    lax.fori_loop(1, count // 8, block, 0)


def greet_all(me):
    barrier = pltpu.get_barrier_semaphore()

    def greet(mask):
        pl.semaphore_signal(
            barrier, inc=1, device_id=(jnp.bitwise_xor(me, mask),), device_id_type=MESH
        )

    spread(DEVICES, 45, greet)
    pl.semaphore_wait(barrier, DEVICES - 1)


def place_at(chip):
    return {"y": chip // 16, "z": lax.rem(chip // 4, 4), "x": lax.rem(chip, 4)}


def shift(at, axis, step):
    moved = dict(at)
    moved[axis] = lax.rem(at[axis] + step + 4, 4)
    return moved


def device_at(at, core):
    return ((at["y"] * 4 + at["z"]) * 4 + at["x"]) * 2 + core


def left_form(value, ref):
    high, low = split(value)
    tail = value[:, 512:RP]
    ref[:, 0:512] = high[:, 0:512]
    ref[:, 512:1024] = high[:, 0:512]
    ref[:, 1024:1536] = low[:, 0:512]
    ref[:, 1536:1664] = (tail + pltpu.roll(tail, 64, 1)).astype(BF16)
    ref[:, 1664:1792] = low[:, 512:RP]


def right_form(value, ref):
    high, low = split(value)
    ref[0:512, :] = high[0:512]
    ref[512:1024, :] = low[0:512]
    ref[1024:1536, :] = high[0:512]
    ref[1536:1600, :] = high[512:R]
    ref[1600:1664, :] = low[512:R]
    ref[1664:1728, :] = high[512:R]


def symmetric_dot(left, right, out):
    c0 = dot(left[...], right[:, 0:256])
    c1 = dot(left[256:R, :], right[:, 256:512])
    c2 = dot(left[512:R, :], right[:, 512:RP])
    blank = jnp.zeros((64, 256), F32)
    out[:, 0:256] = c0
    out[256:R, 256:512] = c1
    out[512:R, 512:RP] = c2
    out[0:256, 256:512] = c0[256:512].T
    out[0:256, 512:RP] = jnp.concatenate([c0[512:R], blank], axis=0).T
    out[256:512, 512:RP] = jnp.concatenate([c1[256:320], blank], axis=0).T


ORDERS = ("xyz", "yzx", "zxy")
OFFSETS = (0, -1, 1, 2)
SIDES = ((0, 1), (1, -1))


def gather_steps(buf, send_a, send_b, recv_a, recv_b, sib_send, sib_recv):
    me, chip, core = position()
    home = place_at(chip)
    sibling = chip * 2 + 1 - core
    parts = range(3)

    def device(at):
        return device_at(at, core)

    def rows_of(part, half):
        row = R * core + 192 * part + (0 if half is None else 96 * half)
        return pl.ds(pl.multiple_of(row, 16), 192 if half is None else 96)

    def tile(part, at):
        y, z, x = at["y"], at["z"], at["x"]
        return jnp.logical_or(y < 3, z < 2), 1, 0, lambda n: (y, z, pl.ds(x, n))

    def line(part, at):
        y, z, x = at["y"], at["z"], at["x"]
        if part == 0:
            return jnp.logical_or(y < 3, z < 2), 4, 0, lambda n: (y, z, pl.ds(0, n))
        if part == 1:
            return z < 2, 4, 3, lambda n: (pl.ds(0, n), z, x)
        return y < 3, 4, 2, lambda n: (y, pl.ds(0, n), x)

    def each(spec, act):
        whole, count, fewer, index = spec

        @pl.when(whole)
        def _():
            act(count, index(count))

        if fewer:

            @pl.when(jnp.logical_not(whole))
            def _():
                act(fewer, index(fewer))

    def push(part, spec, send_sem, recv_sem, to, half=None):
        def act(count, index):
            block = buf.at[(*index, rows_of(part, half))]
            remote(block, block, send_sem, recv_sem, to).start()

        each(spec, act)

    def take(spec, sem, rows=192):
        def act(count, index):
            drain(buf.at[0, 0, pl.ds(0, count), pl.ds(0, rows)], sem)

        each(spec, act)

    def take_halves(first, second, sem):
        def outer(m, _):
            def inner(n, _):
                drain(buf.at[0, 0, 0, pl.ds(0, 96 * (m + n))], sem)

            each(second, inner)
            if not second[2]:

                @pl.when(jnp.logical_not(second[0]))
                def _():
                    drain(buf.at[0, 0, 0, pl.ds(0, 96 * m)], sem)

        each(first, outer)
        if not first[2]:

            @pl.when(jnp.logical_and(jnp.logical_not(first[0]), second[0]))
            def _():
                drain(buf.at[0, 0, 0, pl.ds(0, 96 * second[1])], sem)

    def both(part, k, spec, axis):
        for d, step in SIDES:
            push(part, spec, send_a.at[part, k], recv_a.at[part, k, d], device(shift(home, axis, step)))

    def pass_on(part, k, spec, d, axis, step):
        push(part, spec, send_b.at[part, k], recv_b.at[part, k], device(shift(home, axis, step)), half=d)

    def near(part, axis, step, i):
        return line(part, shift(shift(home, axis, step), ORDERS[part][1], OFFSETS[i]))

    def tell(part, spec):
        push(part, spec, sib_send, sib_recv, sibling)

    def tell_plane(part, at):
        y, z, x = at["y"], at["z"], at["x"]
        every = pl.ds(0, 4)
        if part == 0:
            tell(part, (z < 2, 4, 3, lambda n: (pl.ds(0, n), z, every)))
        elif part == 1:
            tell(part, (x >= 0, 3, 0, lambda n: (pl.ds(0, n), every, x)))
            tell(part, (x >= 0, 2, 0, lambda n: (3, pl.ds(0, n), x)))
        else:
            tell(part, (y < 3, 4, 2, lambda n: (y, pl.ds(0, n), every)))

    def forward(part, i):
        axis = ORDERS[part][2]
        for d, step in SIDES:
            got = near(part, axis, -step, i)
            take(got, recv_a.at[part, 2 + i, d])
            pass_on(part, 2 + i, got, d, axis, step)

    for p in parts:
        own, axis = tile(p, home), ORDERS[p][0]
        both(p, 0, own, axis)
        push(p, own, send_a.at[p, 0], recv_b.at[p, 0], device(shift(home, axis, 2)))
    for p in parts:
        first, second, _ = ORDERS[p]
        for d, step in SIDES:
            take(tile(p, shift(home, first, -step)), recv_a.at[p, 0, d])
        take(tile(p, shift(home, first, 2)), recv_b.at[p, 0])
        both(p, 1, line(p, home), second)
    for p in parts:
        both(p, 2, line(p, home), ORDERS[p][2])
    for p in parts:
        second = ORDERS[p][1]
        for d, step in SIDES:
            got = line(p, shift(home, second, -step))
            take(got, recv_a.at[p, 1, d])
            pass_on(p, 1, got, d, second, step)
    for p in parts:
        _, second, third = ORDERS[p]
        for d, step in SIDES:
            both(p, 3 + d, line(p, shift(home, second, -step)), third)
    for p in parts:
        forward(p, 0)
    for p in parts:
        _, second, third = ORDERS[p]
        got = line(p, shift(home, second, 2))
        take(got, recv_b.at[p, 1])
        both(p, 5, got, third)
    for p in parts:
        tell_plane(p, home)
    for i in (1, 2, 3):
        for p in parts:
            forward(p, i)
    for p in parts:
        for d, step in SIDES:
            tell_plane(p, shift(home, ORDERS[p][2], -step))
    for i in range(4):
        for p in parts:
            got = near(p, ORDERS[p][2], 2, i)
            take(got, recv_b.at[p, 2 + i])
            tell(p, got)

    for p in parts:
        first, second, third = ORDERS[p]
        take(tile(p, home), send_a.at[p, 0], 576)
        take(line(p, home), send_a.at[p, 1], 384)
        take_halves(line(p, shift(home, second, -1)), line(p, shift(home, second, 1)), send_b.at[p, 1])
        for i in range(4):
            take(near(p, third, 0, i), send_a.at[p, 2 + i], 384)
            take_halves(near(p, third, -1, i), near(p, third, 1, i), send_b.at[p, 2 + i])
    for sem in (sib_send, sib_recv):
        drain(buf.at[pl.ds(0, 3), :, :, pl.ds(0, 672)], sem)


def step_kernel(
    out_ref, mom_ref, mine_ref, slot_ref, fresh_ref, buf,
    got, place, columns, packed, terms, partial, terms2, summed, relay, chosen, arrived, mcol,
    gram, gram2, ga, gb, pbs, ta, xa,
    a2a_send, a2a_recv, swap_send, swap_recv, rs1_send, rs2_send, ag1_send, ag2_send,
    h1_send, h1_recv, h2_send, h2_recv, sib_send, sib_recv,
    rs1_recv, rs2_recv, ag1_recv, ag2_recv, send_a, send_b, recv_b, recv_a,
):
    me, chip, core = position()
    greet_all(me)


    def push(mask):
        to = jnp.bitwise_xor(me, mask)
        remote(out_ref.at[to], got.at[me], a2a_send, a2a_recv, to).start()

    spread(DEVICES, 45, push)
    got[pl.ds(me, 1)] = out_ref[pl.ds(me, 1)]
    rows = lax.broadcasted_iota(jnp.int32, (256, 128), 0)
    lanes = lax.broadcasted_iota(jnp.int32, (1, 128), 1)
    for t in range(9):
        row = lanes + 128 * t
        source = lax.shift_right_logical(row * 7282, 16)
        r = row - 9 * source
        half = lax.shift_right_logical(r, 1)
        odd = r - 2 * half
        base = 16 * (source - window_start(t)) + half
        for k in range(3):
            for parity in range(2):
                target = jnp.where(odd == parity, base + 5 * k, -1)
                place[t, :, pl.ds(128 * (2 * k + parity), 128)] = jnp.where(
                    rows == target, 1.0, 0.0
                ).astype(BF16)
    for i in range(ITERS - 1):
        pbs[i, 1728:K3, :] = jnp.zeros((K3 - 1728, RP), BF16)
    gb[1728:K3, :] = jnp.zeros((K3 - 1728, RP), BF16)
    chosen[DEVICES : DEVICES + 2] = jnp.zeros((2, 8, 128), F32)
    others = got.at[pl.ds(0, DEVICES - 1)]
    drain(others, a2a_recv)
    for t in range(9):
        window = got[pl.ds(window_start(t), 16)].reshape(256, 128)
        placed = lax.dot_general(
            window, place[t], (((0,), (0,)), ((), ())), preferred_element_type=F32
        )
        for k in range(3):
            grad = (
                placed[0:56, 256 * k : 256 * k + 128]
                + placed[64:120, 256 * k + 128 : 256 * k + 256]
            )
            fresh_ref[k, :, pl.ds(128 * t, 128)] = (
                0.95 * mom_ref[k, :, pl.ds(128 * t, 128)] + grad
            ) * mine_ref[k]

    sibling = chip * 2 + 1 - core
    mine_lanes = pl.ds(pl.multiple_of(512 * core, 128), RP)
    their_lanes = pl.ds(pl.multiple_of(512 * (1 - core), 128), RP)
    swap = remote(fresh_ref.at[:, :, their_lanes], columns.at[1], swap_send, swap_recv, sibling)
    swap.start()
    columns[0] = fresh_ref[:, :, mine_lanes]
    swap.wait_recv()
    both = align_layer(columns[...].reshape(336, RP), core)
    high, low = split(both)
    gram[...] = lax.dot_general(
        jnp.concatenate([high, high, low], axis=0),
        jnp.concatenate([high, low, high], axis=0),
        (((0,), (0,)), ((), ())),
        preferred_element_type=F32,
    )[0:R]
    pack(gram, packed)

    home = place_at(chip)

    def plane_of(p):
        return home[ORDERS[p][0]] * 4 + home[ORDERS[p][1]]

    def block_of(p, third):
        return pl.ds(pl.multiple_of(512 * p + 128 * third, 8), 128)

    def piece_of(p, plane):
        return pl.ds(pl.multiple_of(512 * p + 128 * home[ORDERS[p][2]] + 8 * plane, 8), 8)

    def plane_peer(p, mask):
        other = jnp.bitwise_xor(plane_of(p), mask)
        at = dict(home)
        at[ORDERS[p][0]] = other // 4
        at[ORDERS[p][1]] = lax.rem(other, 4)
        return other, device_at(at, core)

    for p in range(3):
        third = ORDERS[p][2]
        for step in (1, 2, 3):
            there = shift(home, third, step)
            remote(
                packed.at[block_of(p, there[third])],
                terms.at[p, home[third]],
                rs1_send, rs1_recv.at[p], device_at(there, core),
            ).start()
    for p in range(3):
        third = home[ORDERS[p][2]]
        terms[p, pl.ds(third, 1)] = packed[block_of(p, third)][None]
        drain(packed.at[pl.ds(0, 384)], rs1_recv.at[p])
        partial[p] = jnp.sum(terms[p], axis=0)
        for mask in range(1, 16):
            other, to = plane_peer(p, mask)
            remote(
                partial.at[p, pl.ds(pl.multiple_of(8 * other, 8), 8)],
                terms2.at[p, plane_of(p)],
                rs2_send, rs2_recv.at[p], to,
            ).start()
    for p in range(3):
        plane = plane_of(p)
        terms2[p, pl.ds(plane, 1)] = partial[p, pl.ds(pl.multiple_of(8 * plane, 8), 8)][None]
        drain(packed.at[pl.ds(0, 120)], rs2_recv.at[p])
        summed[piece_of(p, plane)] = jnp.sum(terms2[p], axis=0)
        for mask in range(1, 16):
            _, to = plane_peer(p, mask)
            piece = summed.at[piece_of(p, plane)]
            remote(piece, piece, ag1_send, ag1_recv.at[p], to).start()
    for p in range(3):
        third = ORDERS[p][2]
        drain(packed.at[pl.ds(0, 120)], ag1_recv.at[p])
        block = summed.at[block_of(p, home[third])]
        for step in (1, 2, 3):
            remote(block, block, ag2_send, ag2_recv.at[p], device_at(shift(home, third, step), core)).start()

    def to_relay(i, carry):
        t = i // 7
        q = lax.rem(i, 7)
        to = jnp.where(i < 28, 2 * i + 1, jnp.where(i < 35, 2 * i + 57, 2 * i - 14))
        src = fresh_ref.at[
            :, pl.ds(pl.multiple_of(8 * q, 8), 8), pl.ds(pl.multiple_of(128 * t, 128), 128)
        ]
        dst = relay.at[pl.ds(3 * me, 3)]

        @pl.when(to != me)
        def _():
            remote(src, dst, h1_send, h1_recv, to).start()

        @pl.when(to == me)
        def _():
            pltpu.make_async_copy(src, dst, h1_recv).start()

        return carry

    lax.fori_loop(0, RELAYS, to_relay, 0, unroll=7)

    for p in range(3):
        drain(packed.at[pl.ds(0, 384)], ag2_recv.at[p])
    unpack(summed, gram)
    diag = lax.broadcasted_iota(jnp.int32, (R, RP), 0) == lax.broadcasted_iota(jnp.int32, (R, RP), 1)
    squares = jnp.sum(jnp.where(diag, gram[...], 0.0), axis=(0, 1), keepdims=True)
    inverse = 1.0 / (jnp.sqrt(squares) + epsilon)
    gram[...] = gram[...] * (inverse * inverse)

    def polynomial(i):
        g = gram[...]
        left_form(g, ga)
        right_form(g, gb)
        symmetric_dot(ga, gb, gram2)
        p = coef_b * g + coef_c * gram2[...]
        right_form(jnp.where(diag, p + coef_a, p), pbs.at[i])

    def sweep(i, carry):
        polynomial(i)
        symmetric_dot(ga, pbs.at[i], gram2)
        left_form(gram2[...], ta)
        symmetric_dot(ta, pbs.at[i], gram)
        return carry

    lax.fori_loop(0, 2, sweep, 0)

    spans = jnp.logical_and(core == 1, jnp.logical_and(chip >= 56, chip < 63))
    sole = jnp.where(core == 1, chip < 28, jnp.logical_and(chip >= 28, chip < 56))
    relays = jnp.logical_or(spans, sole)
    u = jnp.where(core == 1, jnp.where(chip < 28, chip, chip - 28), chip + 7)
    lane_tile = u // 7 - 4 * (1 - core)
    q = lax.rem(u, 7)

    def first_block(j, q):
        return (16 * j - q + 6) // 7

    @pl.when(relays)
    def _():
        drain(relay, h1_recv)

        def choose(b, carry):
            chosen[pl.ds(b, 1)] = relay[pl.ds(slot_ref[b], 1)]
            return carry

        lax.fori_loop(0, DEVICES, choose, 0, unroll=8)

        def to_columns(j, carry):
            src = chosen.at[pl.ds(first_block(j, q), 3)]
            remote(src, arrived.at[lane_tile, q], h2_send, h2_recv, j * 2 + 1 - core).start()
            return carry

        lax.fori_loop(0, TILES, to_columns, 0, unroll=8)

        @pl.when(spans)
        def _():
            def to_others(j, carry):
                src = chosen.at[pl.ds(first_block(j, q), 3)]
                remote(src, arrived.at[0, q], h2_send, h2_recv, j * 2 + 1).start()
                return carry

            lax.fori_loop(0, TILES, to_others, 0, unroll=8)

    lax.fori_loop(2, ITERS - 1, sweep, 0)
    right_form(gram[...], gb)

    @pl.when(chip < TILES)
    def _():
        drain(arrived, h2_recv)
        for i in range(16):
            octet = 16 * chip + i
            block = octet // 7
            r = octet - 7 * block
            for t in range(5):
                mcol[8 * i : 8 * i + 8, 128 * t : 128 * t + 128] = arrived[
                    t, r, block - first_block(chip, r)
                ]

    @pl.when(chip >= TILES)
    def _():
        mcol[...] = jnp.zeros_like(mcol)

    value = align_layer(mcol[...], core) * inverse

    def apply(i, value):
        left_form(value, xa)
        return dot(xa[...], pbs[i])

    value = lax.fori_loop(0, ITERS - 1, apply, value)
    left_form(value, xa)
    once = dot(xa[...], gb[...])
    left_form(once, xa)
    twice = dot(xa[...], gb[...])
    value = (coef_a * value + coef_b * once + coef_c * twice) * (0.2 * math.sqrt(max(R, 7168)))
    buf[chip // 16, lax.rem(chip // 4, 4), lax.rem(chip, 4), pl.ds(pl.multiple_of(R * core, 16), R)] = (
        value.T[0:R, :].astype(BF16)
    )
    gather_steps(buf, send_a, send_b, recv_a, recv_b, sib_send, sib_recv)

    drain(others, a2a_send)
    swap.wait_send()
    drain(packed.at[pl.ds(0, 1152)], rs1_send)
    drain(packed.at[pl.ds(0, 360)], rs2_send)
    drain(packed.at[pl.ds(0, 360)], ag1_send)
    drain(packed.at[pl.ds(0, 1152)], ag2_send)

    @pl.when(relays)
    def _():
        drain(relay.at[pl.ds(0, 3 * (RELAYS - 1))], h1_send)

    @pl.when(jnp.logical_not(relays))
    def _():
        drain(relay.at[pl.ds(0, 3 * RELAYS)], h1_send)

    @pl.when(sole)
    def _():
        drain(relay.at[pl.ds(0, 3 * TILES)], h2_send)

    @pl.when(spans)
    def _():
        drain(relay.at[pl.ds(0, 6 * TILES)], h2_send)


def step(outgoing, momentum, mine, slot_index):
    return pl.pallas_call(
        step_kernel,
        out_shape=(
            pltpu.VMEM(momentum.shape, F32),
            pltpu.VMEM((4, 4, 4, 2 * R, 128), BF16),
        ),
        in_specs=[
            pl.BlockSpec(memory_space=pltpu.VMEM),
            pl.BlockSpec(memory_space=pltpu.VMEM),
            pl.BlockSpec(memory_space=pltpu.SMEM),
            pl.BlockSpec(memory_space=pltpu.SMEM),
        ],
        out_specs=(
            pl.BlockSpec(memory_space=pltpu.VMEM),
            pl.BlockSpec(memory_space=pltpu.VMEM),
        ),
        scratch_shapes=[
            pltpu.VMEM((DEVICES, 16, 128), BF16),
            pltpu.VMEM((9, 256, 768), BF16),
            pltpu.VMEM((2, 3, 56, RP), F32),
            pltpu.VMEM((1536, 128), F32),
            pltpu.VMEM((3, 4, 128, 128), F32),
            pltpu.VMEM((3, 128, 128), F32),
            pltpu.VMEM((3, 16, 8, 128), F32),
            pltpu.VMEM((1536, 128), F32),
            pltpu.VMEM((384, 8, 128), F32),
            pltpu.VMEM((DEVICES + 2, 8, 128), F32),
            pltpu.VMEM((5, 7, 3, 8, 128), F32),
            pltpu.VMEM((128, RP), F32),
            pltpu.VMEM((R, RP), F32),
            pltpu.VMEM((R, RP), F32),
            pltpu.VMEM((R, K3), BF16),
            pltpu.VMEM((K3, RP), BF16),
            pltpu.VMEM((ITERS - 1, K3, RP), BF16),
            pltpu.VMEM((R, K3), BF16),
            pltpu.VMEM((128, K3), BF16),
        ]
        + [pltpu.SemaphoreType.DMA] * 14
        + [pltpu.SemaphoreType.DMA((3,))] * 4
        + [pltpu.SemaphoreType.DMA((3, 6))] * 3
        + [pltpu.SemaphoreType.DMA((3, 6, 2))],
        compiler_params=pltpu.CompilerParams(
            collective_id=0, has_side_effects=True, vmem_limit_bytes=40 * 2**20
        ),
        name="step",
    )(outgoing, momentum, mine, slot_index)


def place_kernel(buf, fresh, update, momentum, sem):
    copies = [
        pltpu.make_async_copy(
            buf.at[j // 16, j // 4 % 4, j % 4], update.at[:, pl.ds(128 * j, 128)], sem.at[j]
        )
        for j in range(TILES)
    ]
    copies.append(pltpu.make_async_copy(fresh, momentum, sem.at[TILES]))
    for copy in copies:
        copy.start()
    for copy in copies:
        copy.wait()


def place_results(buf, fresh):
    return pl.pallas_call(
        place_kernel,
        out_shape=(
            jax.ShapeDtypeStruct((2 * R, 128 * TILES), BF16),
            jax.ShapeDtypeStruct(fresh.shape, F32),
        ),
        in_specs=[pl.BlockSpec(memory_space=pl.ANY)] * 2,
        out_specs=(pl.BlockSpec(memory_space=pl.ANY),) * 2,
        scratch_shapes=[pltpu.SemaphoreType.DMA((TILES + 1,))],
        compiler_params=pltpu.CompilerParams(vmem_limit_bytes=2 * 2**20),
        name="place",
    )(buf, fresh)


def slot_of_blocks(table, slot_count):
    positions = jnp.arange(table.shape[0], dtype=jnp.int32)
    matching = (table[None, :] == table[:, None]) & (positions[None, :] < positions[:, None])
    ranking = jnp.sum(matching.astype(jnp.int32), axis=1)
    return table * slot_count + ranking


def local(grads, momentum, table):
    me = lax.axis_index("dp")
    slot_index = slot_of_blocks(table, 3)
    hits = slot_index[None, :] == jnp.arange(384, dtype=jnp.int32)[:, None]
    count = jnp.sum((table == me).astype(jnp.int32))
    mine = (jnp.arange(3, dtype=jnp.int32) < count).astype(F32)
    pieces = jnp.pad(grads.reshape(9, 128, 56), ((0, 1), (0, 0), (0, 8)))
    pieces = pieces.transpose(1, 0, 2).reshape(128, 640)
    outgoing = jnp.dot(hits.astype(BF16), pieces, preferred_element_type=F32).astype(BF16)
    outgoing = jnp.pad(outgoing.reshape(128, 15, 128), ((0, 0), (0, 1), (0, 0)))
    fresh, buf = step(outgoing, momentum, mine, slot_index)
    return place_results(buf, fresh)


def solution(mesh):
    in_specs = (P("dp", None), P("dp", None, None), P())
    out_specs = (P(), P("dp", None, None))
    return jax.shard_map(local, mesh=mesh, in_specs=in_specs, out_specs=out_specs, check_vma=False)
```

```python
import math

import jax
import jax.numpy as jnp
from jax import lax
from jax.experimental import pallas as pl
from jax.experimental.pallas import tpu as pltpu
from jax.sharding import PartitionSpec as P

R = 576
ITERS = 5
RP = 640
K3 = 1792
DEVICES = 128
CHIPS = 64
TILES = 56
RELAYS = 63
MESH = pl.DeviceIdType.MESH
F32 = jnp.float32
BF16 = jnp.bfloat16

coef_a = 3.4445
coef_b = -4.775
coef_c = 2.0315
epsilon = 1e-07


def position():
    me = lax.axis_index("dp")
    return me, me // 2, lax.rem(me, 2)


def remote(src, dst, send, recv, to):
    return pltpu.make_async_remote_copy(
        src, dst, send, recv, device_id=(to,), device_id_type=MESH
    )


def drain(view, sem):
    pltpu.make_async_copy(view, view, sem).wait()


def split(value):
    high = value.astype(BF16)
    return high, (value - high.astype(F32)).astype(BF16)


def dot(a, b):
    return jnp.dot(a, b, preferred_element_type=F32)


def window_start(t):
    return min(128 * t // 9, DEVICES - 16)


def align_layer(value, core):
    moved = pltpu.roll(value, (RP - 64) * core, 1)
    lane = lax.broadcasted_iota(jnp.int32, value.shape, 1)
    return jnp.where(lane < R, moved, 0.0)


STRIP = (0, 576, 1024, 1344)


def pack(gram, packed):
    lane = lax.broadcasted_iota(jnp.int32, (64, 128), 1)
    corner = pltpu.roll(gram[512:576, 512:640], 64, 1)
    packed[0:64, :] = jnp.where(lane < 64, gram[0:64, 0:128], corner)
    packed[64:576, :] = gram[64:576, 0:128]
    for s in range(1, 4):
        packed[STRIP[s] : STRIP[s] + 576 - 128 * s, :] = gram[
            128 * s : 576, 128 * s : 128 * s + 128
        ]


def unpack(packed, gram):
    row = lax.broadcasted_iota(jnp.int32, (128, 128), 0)
    lane = lax.broadcasted_iota(jnp.int32, (128, 128), 1)
    upper = (row < 64) & (lane >= 64)
    first = packed[0:128, :]
    clean = jnp.where(upper, 0.0, first)
    gram[0:128, 0:128] = jnp.where(upper, clean.T, clean)
    corner = pltpu.roll(packed[0:64, :], 64, 1)
    lane64 = lax.broadcasted_iota(jnp.int32, (64, 128), 1)
    gram[512:576, 512:640] = jnp.where(lane64 < 64, corner, 0.0)
    for s in range(4):
        for b in range(s, 5):
            if b == s:
                if s:
                    gram[128 * s : 128 * s + 128, 128 * s : 128 * s + 128] = packed[
                        STRIP[s] : STRIP[s] + 128, :
                    ]
                continue
            n = 64 if b == 4 else 128
            start = STRIP[s] + 128 * (b - s)
            block = packed[start : start + n, :]
            gram[128 * b : 128 * b + n, 128 * s : 128 * s + 128] = block
            if n == 64:
                block = jnp.concatenate([block, jnp.zeros((64, 128), F32)], axis=0)
            gram[128 * s : 128 * s + 128, 128 * b : 128 * b + 128] = block.T


def spread(count, factor, act):
    for i in range(1, 8):
        act((i * factor) % count)

    def block(b, carry):
        for i in range(8):
            act(jnp.bitwise_and((8 * b + i) * factor, count - 1))
        return carry

    lax.fori_loop(1, count // 8, block, 0)


def greet_all(me):
    barrier = pltpu.get_barrier_semaphore()

    def greet(mask):
        pl.semaphore_signal(
            barrier, inc=1, device_id=(jnp.bitwise_xor(me, mask),), device_id_type=MESH
        )

    spread(DEVICES, 45, greet)
    return lambda: pl.semaphore_wait(barrier, DEVICES - 1)


def place_at(chip):
    return {"y": chip // 16, "z": lax.rem(chip // 4, 4), "x": lax.rem(chip, 4)}


def shift(at, axis, step):
    moved = dict(at)
    moved[axis] = lax.rem(at[axis] + step + 4, 4)
    return moved


def device_at(at, core):
    return ((at["y"] * 4 + at["z"]) * 4 + at["x"]) * 2 + core


def left_form(value, ref):
    high, low = split(value)
    tail = value[:, 512:RP]
    ref[:, 0:512] = high[:, 0:512]
    ref[:, 512:1024] = high[:, 0:512]
    ref[:, 1024:1536] = low[:, 0:512]
    ref[:, 1536:1664] = (tail + pltpu.roll(tail, 64, 1)).astype(BF16)
    ref[:, 1664:1792] = low[:, 512:RP]


def right_form(value, ref):
    high, low = split(value)
    ref[0:512, :] = high[0:512]
    ref[512:1024, :] = low[0:512]
    ref[1024:1536, :] = high[0:512]
    ref[1536:1600, :] = high[512:R]
    ref[1600:1664, :] = low[512:R]
    ref[1664:1728, :] = high[512:R]


def symmetric_dot(left, right, out):
    c0 = dot(left[...], right[:, 0:256])
    c1 = dot(left[256:R, :], right[:, 256:512])
    c2 = dot(left[512:R, :], right[:, 512:RP])
    blank = jnp.zeros((64, 256), F32)
    out[:, 0:256] = c0
    out[256:R, 256:512] = c1
    out[512:R, 512:RP] = c2
    out[0:256, 256:512] = c0[256:512].T
    out[0:256, 512:RP] = jnp.concatenate([c0[512:R], blank], axis=0).T
    out[256:512, 512:RP] = jnp.concatenate([c1[256:320], blank], axis=0).T


ORDERS = ("xyz", "yzx", "zxy")
OFFSETS = (0, -1, 1, 2)
SIDES = ((0, 1), (1, -1))


def gather_steps(buf, send_a, send_b, recv_a, recv_b, sib_send, sib_recv):
    me, chip, core = position()
    home = place_at(chip)
    sibling = chip * 2 + 1 - core
    parts = range(3)

    def device(at):
        return device_at(at, core)

    def rows_of(part, half):
        row = R * core + 192 * part + (0 if half is None else 96 * half)
        return pl.ds(pl.multiple_of(row, 16), 192 if half is None else 96)

    def tile(part, at):
        y, z, x = at["y"], at["z"], at["x"]
        return jnp.logical_or(y < 3, z < 2), 1, 0, lambda n: (y, z, pl.ds(x, n))

    def line(part, at):
        y, z, x = at["y"], at["z"], at["x"]
        if part == 0:
            return jnp.logical_or(y < 3, z < 2), 4, 0, lambda n: (y, z, pl.ds(0, n))
        if part == 1:
            return z < 2, 4, 3, lambda n: (pl.ds(0, n), z, x)
        return y < 3, 4, 2, lambda n: (y, pl.ds(0, n), x)

    def each(spec, act):
        whole, count, fewer, index = spec

        @pl.when(whole)
        def _():
            act(count, index(count))

        if fewer:

            @pl.when(jnp.logical_not(whole))
            def _():
                act(fewer, index(fewer))

    def push(part, spec, send_sem, recv_sem, to, half=None):
        def act(count, index):
            block = buf.at[(*index, rows_of(part, half))]
            remote(block, block, send_sem, recv_sem, to).start()

        each(spec, act)

    def take(spec, sem, rows=192):
        def act(count, index):
            drain(buf.at[0, 0, pl.ds(0, count), pl.ds(0, rows)], sem)

        each(spec, act)

    def take_halves(first, second, sem):
        def outer(m, _):
            def inner(n, _):
                drain(buf.at[0, 0, 0, pl.ds(0, 96 * (m + n))], sem)

            each(second, inner)
            if not second[2]:

                @pl.when(jnp.logical_not(second[0]))
                def _():
                    drain(buf.at[0, 0, 0, pl.ds(0, 96 * m)], sem)

        each(first, outer)
        if not first[2]:

            @pl.when(jnp.logical_and(jnp.logical_not(first[0]), second[0]))
            def _():
                drain(buf.at[0, 0, 0, pl.ds(0, 96 * second[1])], sem)

    def both(part, k, spec, axis):
        for d, step in SIDES:
            push(part, spec, send_a.at[part, k], recv_a.at[part, k, d], device(shift(home, axis, step)))

    def pass_on(part, k, spec, d, axis, step):
        push(part, spec, send_b.at[part, k], recv_b.at[part, k], device(shift(home, axis, step)), half=d)

    def near(part, axis, step, i):
        return line(part, shift(shift(home, axis, step), ORDERS[part][1], OFFSETS[i]))

    def tell(part, spec):
        push(part, spec, sib_send, sib_recv, sibling)

    def tell_plane(part, at):
        y, z, x = at["y"], at["z"], at["x"]
        every = pl.ds(0, 4)
        if part == 0:
            tell(part, (z < 2, 4, 3, lambda n: (pl.ds(0, n), z, every)))
        elif part == 1:
            tell(part, (x >= 0, 3, 0, lambda n: (pl.ds(0, n), every, x)))
            tell(part, (x >= 0, 2, 0, lambda n: (3, pl.ds(0, n), x)))
        else:
            tell(part, (y < 3, 4, 2, lambda n: (y, pl.ds(0, n), every)))

    def forward(part, i):
        axis = ORDERS[part][2]
        for d, step in SIDES:
            got = near(part, axis, -step, i)
            take(got, recv_a.at[part, 2 + i, d])
            pass_on(part, 2 + i, got, d, axis, step)

    for p in parts:
        own, axis = tile(p, home), ORDERS[p][0]
        both(p, 0, own, axis)
        push(p, own, send_a.at[p, 0], recv_b.at[p, 0], device(shift(home, axis, 2)))
    for p in parts:
        first, second, _ = ORDERS[p]
        for d, step in SIDES:
            take(tile(p, shift(home, first, -step)), recv_a.at[p, 0, d])
        take(tile(p, shift(home, first, 2)), recv_b.at[p, 0])
        both(p, 1, line(p, home), second)
    for p in parts:
        both(p, 2, line(p, home), ORDERS[p][2])
    for p in parts:
        second = ORDERS[p][1]
        for d, step in SIDES:
            got = line(p, shift(home, second, -step))
            take(got, recv_a.at[p, 1, d])
            pass_on(p, 1, got, d, second, step)
    for p in parts:
        _, second, third = ORDERS[p]
        for d, step in SIDES:
            both(p, 3 + d, line(p, shift(home, second, -step)), third)
    for p in parts:
        forward(p, 0)
    for p in parts:
        _, second, third = ORDERS[p]
        got = line(p, shift(home, second, 2))
        take(got, recv_b.at[p, 1])
        both(p, 5, got, third)
    for p in parts:
        tell_plane(p, home)
    for i in (1, 2, 3):
        for p in parts:
            forward(p, i)
    for p in parts:
        for d, step in SIDES:
            tell_plane(p, shift(home, ORDERS[p][2], -step))
    for i in range(4):
        for p in parts:
            got = near(p, ORDERS[p][2], 2, i)
            take(got, recv_b.at[p, 2 + i])
            tell(p, got)

    for p in parts:
        first, second, third = ORDERS[p]
        take(tile(p, home), send_a.at[p, 0], 576)
        take(line(p, home), send_a.at[p, 1], 384)
        take_halves(line(p, shift(home, second, -1)), line(p, shift(home, second, 1)), send_b.at[p, 1])
        for i in range(4):
            take(near(p, third, 0, i), send_a.at[p, 2 + i], 384)
            take_halves(near(p, third, -1, i), near(p, third, 1, i), send_b.at[p, 2 + i])
    for sem in (sib_send, sib_recv):
        drain(buf.at[pl.ds(0, 3), :, :, pl.ds(0, 672)], sem)


def step_kernel(
    pieces_ref, mom_ref, table_ref, fresh_ref, buf,
    hits, outgoing, slot_row, slots, got, place, columns, packed, terms, partial, terms2, summed, relay, chosen, arrived, mcol,
    gram, gram2, ga, gb, pbs, ta, xa,
    a2a_send, a2a_recv, swap_send, swap_recv, rs1_send, rs2_send, ag1_send, ag2_send,
    h1_send, h1_recv, h2_send, h2_recv, sib_send, sib_recv, slot_sem,
    rs1_recv, rs2_recv, ag1_recv, ag2_recv, send_a, send_b, recv_b, recv_a,
):
    me, chip, core = position()
    greeted = greet_all(me)

    table = table_ref[...].astype(F32)
    owners = jnp.broadcast_to(table, (DEVICES, DEVICES))
    sub = lax.broadcasted_iota(jnp.int32, (DEVICES, DEVICES), 0)
    lane = lax.broadcasted_iota(jnp.int32, (DEVICES, DEVICES), 1)
    earlier = jnp.logical_and(owners == owners.T, sub < lane)
    rank = jnp.sum(jnp.where(earlier, 1.0, 0.0), axis=0, keepdims=True)
    slot_row[...] = (3.0 * table + rank).astype(jnp.int32)
    slot_copy = pltpu.make_async_copy(slot_row, slots, slot_sem)
    slot_copy.start()
    owned = jnp.sum(jnp.where(table == me.astype(F32), 1.0, 0.0), axis=1, keepdims=True)
    line = (16.0 * table + 5.0 * rank).astype(jnp.int32)
    lines = lax.broadcasted_iota(jnp.int32, (16 * DEVICES, DEVICES), 0)
    for i in range(5):
        hits[:, 128 * i : 128 * i + 128] = jnp.where(lines == line + i, 1.0, 0.0).astype(BF16)
    outgoing[...] = dot(hits[...], pieces_ref[...]).astype(BF16).reshape(DEVICES, 16, 128)
    slot_copy.wait()
    greeted()


    def push(mask):
        to = jnp.bitwise_xor(me, mask)
        remote(outgoing.at[to], got.at[me], a2a_send, a2a_recv, to).start()

    spread(DEVICES, 45, push)
    got[pl.ds(me, 1)] = outgoing[pl.ds(me, 1)]
    rows = lax.broadcasted_iota(jnp.int32, (256, 128), 0)
    lanes = lax.broadcasted_iota(jnp.int32, (1, 128), 1)
    for t in range(9):
        row = lanes + 128 * t
        source = lax.shift_right_logical(row * 7282, 16)
        r = row - 9 * source
        half = lax.shift_right_logical(r, 1)
        odd = r - 2 * half
        base = 16 * (source - window_start(t)) + half
        for k in range(3):
            for parity in range(2):
                target = jnp.where(odd == parity, base + 5 * k, -1)
                place[t, :, pl.ds(128 * (2 * k + parity), 128)] = jnp.where(
                    rows == target, 1.0, 0.0
                ).astype(BF16)
    for i in range(ITERS - 1):
        pbs[i, 1728:K3, :] = jnp.zeros((K3 - 1728, RP), BF16)
    gb[1728:K3, :] = jnp.zeros((K3 - 1728, RP), BF16)
    chosen[DEVICES : DEVICES + 2] = jnp.zeros((2, 8, 128), F32)
    others = got.at[pl.ds(0, DEVICES - 1)]
    drain(others, a2a_recv)
    for t in range(9):
        window = got[pl.ds(window_start(t), 16)].reshape(256, 128)
        placed = lax.dot_general(
            window, place[t], (((0,), (0,)), ((), ())), preferred_element_type=F32
        )
        for k in range(3):
            grad = (
                placed[0:56, 256 * k : 256 * k + 128]
                + placed[64:120, 256 * k + 128 : 256 * k + 256]
            )
            fresh_ref[k, :, pl.ds(128 * t, 128)] = (
                0.95 * mom_ref[k, :, pl.ds(128 * t, 128)] + grad
            ) * jnp.where(owned > k, 1.0, 0.0)

    sibling = chip * 2 + 1 - core
    mine_lanes = pl.ds(pl.multiple_of(512 * core, 128), RP)
    their_lanes = pl.ds(pl.multiple_of(512 * (1 - core), 128), RP)
    swap = remote(fresh_ref.at[:, :, their_lanes], columns.at[1], swap_send, swap_recv, sibling)
    swap.start()
    columns[0] = fresh_ref[:, :, mine_lanes]
    swap.wait_recv()
    both = align_layer(columns[...].reshape(336, RP), core)
    high, low = split(both)
    gram[...] = lax.dot_general(
        jnp.concatenate([high, high, low], axis=0),
        jnp.concatenate([high, low, high], axis=0),
        (((0,), (0,)), ((), ())),
        preferred_element_type=F32,
    )[0:R]
    pack(gram, packed)

    home = place_at(chip)

    def plane_of(p):
        return home[ORDERS[p][0]] * 4 + home[ORDERS[p][1]]

    def block_of(p, third):
        return pl.ds(pl.multiple_of(512 * p + 128 * third, 8), 128)

    def piece_of(p, plane):
        return pl.ds(pl.multiple_of(512 * p + 128 * home[ORDERS[p][2]] + 8 * plane, 8), 8)

    def plane_peer(p, mask):
        other = jnp.bitwise_xor(plane_of(p), mask)
        at = dict(home)
        at[ORDERS[p][0]] = other // 4
        at[ORDERS[p][1]] = lax.rem(other, 4)
        return other, device_at(at, core)

    for p in range(3):
        third = ORDERS[p][2]
        for step in (1, 2, 3):
            there = shift(home, third, step)
            remote(
                packed.at[block_of(p, there[third])],
                terms.at[p, home[third]],
                rs1_send, rs1_recv.at[p], device_at(there, core),
            ).start()
    for p in range(3):
        third = home[ORDERS[p][2]]
        terms[p, pl.ds(third, 1)] = packed[block_of(p, third)][None]
        drain(packed.at[pl.ds(0, 384)], rs1_recv.at[p])
        partial[p] = jnp.sum(terms[p], axis=0)
        for mask in range(1, 16):
            other, to = plane_peer(p, mask)
            remote(
                partial.at[p, pl.ds(pl.multiple_of(8 * other, 8), 8)],
                terms2.at[p, plane_of(p)],
                rs2_send, rs2_recv.at[p], to,
            ).start()
    for p in range(3):
        plane = plane_of(p)
        terms2[p, pl.ds(plane, 1)] = partial[p, pl.ds(pl.multiple_of(8 * plane, 8), 8)][None]
        drain(packed.at[pl.ds(0, 120)], rs2_recv.at[p])
        summed[piece_of(p, plane)] = jnp.sum(terms2[p], axis=0)
        for mask in range(1, 16):
            _, to = plane_peer(p, mask)
            piece = summed.at[piece_of(p, plane)]
            remote(piece, piece, ag1_send, ag1_recv.at[p], to).start()
    for p in range(3):
        third = ORDERS[p][2]
        drain(packed.at[pl.ds(0, 120)], ag1_recv.at[p])
        block = summed.at[block_of(p, home[third])]
        for step in (1, 2, 3):
            remote(block, block, ag2_send, ag2_recv.at[p], device_at(shift(home, third, step), core)).start()

    def to_relay(n, carry):
        i = lax.rem(n + 28, RELAYS)
        t = i // 7
        q = lax.rem(i, 7)
        to = jnp.where(i < 28, 2 * i + 1, jnp.where(i < 35, 2 * i + 57, 2 * i - 14))
        src = fresh_ref.at[
            :, pl.ds(pl.multiple_of(8 * q, 8), 8), pl.ds(pl.multiple_of(128 * t, 128), 128)
        ]
        dst = relay.at[pl.ds(3 * me, 3)]

        @pl.when(to != me)
        def _():
            remote(src, dst, h1_send, h1_recv, to).start()

        @pl.when(to == me)
        def _():
            pltpu.make_async_copy(src, dst, h1_recv).start()

        return carry

    lax.fori_loop(0, RELAYS, to_relay, 0, unroll=7)

    for p in range(3):
        drain(packed.at[pl.ds(0, 384)], ag2_recv.at[p])
    unpack(summed, gram)
    spans = jnp.logical_and(core == 1, jnp.logical_and(chip >= 56, chip < 63))
    sole = jnp.where(core == 1, chip < 28, jnp.logical_and(chip >= 28, chip < 56))
    relays = jnp.logical_or(spans, sole)
    u = jnp.where(core == 1, jnp.where(chip < 28, chip, chip - 28), chip + 7)
    lane_tile = u // 7 - 4 * (1 - core)
    q = lax.rem(u, 7)

    def first_block(j, q):
        return (16 * j - q + 6) // 7

    def relay_blocks():
        drain(relay, h1_recv)

        def choose(b, carry):
            chosen[pl.ds(b, 1)] = relay[pl.ds(jnp.clip(slots[0, b], 0, 383), 1)]
            return carry

        lax.fori_loop(0, DEVICES, choose, 0, unroll=8)

    def send_columns(tile, layer):
        def to_columns(j, carry):
            src = chosen.at[pl.ds(first_block(j, q), 3)]
            remote(src, arrived.at[tile, q], h2_send, h2_recv, j * 2 + layer).start()
            return carry

        lax.fori_loop(0, TILES, to_columns, 0, unroll=8)

    @pl.when(spans)
    def _():
        relay_blocks()
        send_columns(4, 0)
        send_columns(0, 1)

    diag = lax.broadcasted_iota(jnp.int32, (R, RP), 0) == lax.broadcasted_iota(jnp.int32, (R, RP), 1)
    squares = jnp.sum(jnp.where(diag, gram[...], 0.0), axis=(0, 1), keepdims=True)
    inverse = 1.0 / (jnp.sqrt(squares) + epsilon)
    gram[...] = gram[...] * (inverse * inverse)

    def polynomial(i):
        g = gram[...]
        left_form(g, ga)
        right_form(g, gb)
        symmetric_dot(ga, gb, gram2)
        p = coef_b * g + coef_c * gram2[...]
        right_form(jnp.where(diag, p + coef_a, p), pbs.at[i])

    def sweep(i, carry):
        polynomial(i)
        symmetric_dot(ga, pbs.at[i], gram2)
        left_form(gram2[...], ta)
        symmetric_dot(ta, pbs.at[i], gram)
        return carry

    lax.fori_loop(0, 2, sweep, 0)

    @pl.when(sole)
    def _():
        relay_blocks()
        send_columns(lane_tile, 1 - core)

    lax.fori_loop(2, ITERS - 1, sweep, 0)
    right_form(gram[...], gb)

    @pl.when(chip < TILES)
    def _():
        drain(arrived, h2_recv)
        for i in range(16):
            octet = 16 * chip + i
            block = octet // 7
            r = octet - 7 * block
            for t in range(5):
                mcol[8 * i : 8 * i + 8, 128 * t : 128 * t + 128] = arrived[
                    t, r, block - first_block(chip, r)
                ]

    @pl.when(chip >= TILES)
    def _():
        mcol[...] = jnp.zeros_like(mcol)

    value = align_layer(mcol[...], core) * inverse

    def apply(i, value):
        left_form(value, xa)
        return dot(xa[...], pbs[i])

    value = lax.fori_loop(0, ITERS - 1, apply, value)
    left_form(value, xa)
    once = dot(xa[...], gb[...])
    left_form(once, xa)
    twice = dot(xa[...], gb[...])
    value = (coef_a * value + coef_b * once + coef_c * twice) * (0.2 * math.sqrt(max(R, 7168)))
    buf[chip // 16, lax.rem(chip // 4, 4), lax.rem(chip, 4), pl.ds(pl.multiple_of(R * core, 16), R)] = (
        value.T[0:R, :].astype(BF16)
    )
    gather_steps(buf, send_a, send_b, recv_a, recv_b, sib_send, sib_recv)

    drain(others, a2a_send)
    swap.wait_send()
    drain(packed.at[pl.ds(0, 1152)], rs1_send)
    drain(packed.at[pl.ds(0, 360)], rs2_send)
    drain(packed.at[pl.ds(0, 360)], ag1_send)
    drain(packed.at[pl.ds(0, 1152)], ag2_send)

    @pl.when(relays)
    def _():
        drain(relay.at[pl.ds(0, 3 * (RELAYS - 1))], h1_send)

    @pl.when(jnp.logical_not(relays))
    def _():
        drain(relay.at[pl.ds(0, 3 * RELAYS)], h1_send)

    @pl.when(sole)
    def _():
        drain(relay.at[pl.ds(0, 3 * TILES)], h2_send)

    @pl.when(spans)
    def _():
        drain(relay.at[pl.ds(0, 6 * TILES)], h2_send)


def step(pieces, momentum, table):
    return pl.pallas_call(
        step_kernel,
        out_shape=(
            pltpu.VMEM(momentum.shape, F32),
            pltpu.VMEM((4, 4, 4, 2 * R, 128), BF16),
        ),
        in_specs=[
            pl.BlockSpec(memory_space=pltpu.VMEM),
            pl.BlockSpec(memory_space=pltpu.VMEM),
            pl.BlockSpec(memory_space=pltpu.VMEM),
        ],
        out_specs=(
            pl.BlockSpec(memory_space=pltpu.VMEM),
            pl.BlockSpec(memory_space=pltpu.VMEM),
        ),
        scratch_shapes=[
            pltpu.VMEM((16 * DEVICES, 5 * 128), BF16),
            pltpu.VMEM((DEVICES, 16, 128), BF16),
            pltpu.VMEM((1, DEVICES), jnp.int32),
            pltpu.SMEM((1, DEVICES), jnp.int32),
            pltpu.VMEM((DEVICES, 16, 128), BF16),
            pltpu.VMEM((9, 256, 768), BF16),
            pltpu.VMEM((2, 3, 56, RP), F32),
            pltpu.VMEM((1536, 128), F32),
            pltpu.VMEM((3, 4, 128, 128), F32),
            pltpu.VMEM((3, 128, 128), F32),
            pltpu.VMEM((3, 16, 8, 128), F32),
            pltpu.VMEM((1536, 128), F32),
            pltpu.VMEM((384, 8, 128), F32),
            pltpu.VMEM((DEVICES + 2, 8, 128), F32),
            pltpu.VMEM((5, 7, 3, 8, 128), F32),
            pltpu.VMEM((128, RP), F32),
            pltpu.VMEM((R, RP), F32),
            pltpu.VMEM((R, RP), F32),
            pltpu.VMEM((R, K3), BF16),
            pltpu.VMEM((K3, RP), BF16),
            pltpu.VMEM((ITERS - 1, K3, RP), BF16),
            pltpu.VMEM((R, K3), BF16),
            pltpu.VMEM((128, K3), BF16),
        ]
        + [pltpu.SemaphoreType.DMA] * 15
        + [pltpu.SemaphoreType.DMA((3,))] * 4
        + [pltpu.SemaphoreType.DMA((3, 6))] * 3
        + [pltpu.SemaphoreType.DMA((3, 6, 2))],
        compiler_params=pltpu.CompilerParams(
            collective_id=0, has_side_effects=True, vmem_limit_bytes=40 * 2**20
        ),
        name="step",
    )(pieces, momentum, table)


def place_kernel(buf, fresh, update, momentum, sem):
    copies = [
        pltpu.make_async_copy(
            buf.at[j // 16, j // 4 % 4, j % 4], update.at[:, pl.ds(128 * j, 128)], sem.at[j]
        )
        for j in range(TILES)
    ]
    copies.append(pltpu.make_async_copy(fresh, momentum, sem.at[TILES]))
    for copy in copies:
        copy.start()
    for copy in copies:
        copy.wait()


def place_results(buf, fresh):
    return pl.pallas_call(
        place_kernel,
        out_shape=(
            jax.ShapeDtypeStruct((2 * R, 128 * TILES), BF16),
            jax.ShapeDtypeStruct(fresh.shape, F32),
        ),
        in_specs=[pl.BlockSpec(memory_space=pl.ANY)] * 2,
        out_specs=(pl.BlockSpec(memory_space=pl.ANY),) * 2,
        scratch_shapes=[pltpu.SemaphoreType.DMA((TILES + 1,))],
        compiler_params=pltpu.CompilerParams(vmem_limit_bytes=2 * 2**20),
        name="place",
    )(buf, fresh)


def local(grads, momentum, table):
    pieces = jnp.pad(grads.reshape(9, 128, 56), ((0, 1), (0, 0), (0, 8)))
    pieces = pieces.reshape(5, 2, 128, 64).transpose(0, 2, 1, 3).reshape(640, 128)
    fresh, buf = step(pieces, momentum, table.reshape(1, DEVICES))
    return place_results(buf, fresh)


def solution(mesh):
    in_specs = (P("dp", None), P("dp", None, None), P())
    out_specs = (P(), P("dp", None, None))
    return jax.shard_map(local, mesh=mesh, in_specs=in_specs, out_specs=out_specs, check_vma=False)
```

```python
import math

import jax
import jax.numpy as jnp
from jax import lax
from jax.experimental import pallas as pl
from jax.experimental.pallas import tpu as pltpu
from jax.sharding import PartitionSpec as P

R = 576
ITERS = 5
RP = 640
K3 = 1792
DEVICES = 128
CHIPS = 64
TILES = 56
RELAYS = 63
MESH = pl.DeviceIdType.MESH
F32 = jnp.float32
BF16 = jnp.bfloat16

coef_a = 3.4445
coef_b = -4.775
coef_c = 2.0315
epsilon = 1e-07


def position():
    me = lax.axis_index("dp")
    return me, me // 2, lax.rem(me, 2)


def remote(src, dst, send, recv, to):
    return pltpu.make_async_remote_copy(
        src, dst, send, recv, device_id=(to,), device_id_type=MESH
    )


def drain(view, sem):
    pltpu.make_async_copy(view, view, sem).wait()


def split(value):
    high = value.astype(BF16)
    return high, (value - high.astype(F32)).astype(BF16)


def dot(a, b):
    return jnp.dot(a, b, preferred_element_type=F32)


def window_start(t):
    return min(128 * t // 9, DEVICES - 16)


def align_layer(value, core):
    moved = pltpu.roll(value, (RP - 64) * core, 1)
    lane = lax.broadcasted_iota(jnp.int32, value.shape, 1)
    return jnp.where(lane < R, moved, 0.0)


STRIP = (0, 576, 1024, 1344)


def pack(gram, packed):
    lane = lax.broadcasted_iota(jnp.int32, (64, 128), 1)
    corner = pltpu.roll(gram[512:576, 512:640], 64, 1)
    packed[0:64, :] = jnp.where(lane < 64, gram[0:64, 0:128], corner)
    packed[64:576, :] = gram[64:576, 0:128]
    for s in range(1, 4):
        packed[STRIP[s] : STRIP[s] + 576 - 128 * s, :] = gram[
            128 * s : 576, 128 * s : 128 * s + 128
        ]


def unpack(packed, gram):
    row = lax.broadcasted_iota(jnp.int32, (128, 128), 0)
    lane = lax.broadcasted_iota(jnp.int32, (128, 128), 1)
    upper = (row < 64) & (lane >= 64)
    first = packed[0:128, :]
    clean = jnp.where(upper, 0.0, first)
    gram[0:128, 0:128] = jnp.where(upper, clean.T, clean)
    corner = pltpu.roll(packed[0:64, :], 64, 1)
    lane64 = lax.broadcasted_iota(jnp.int32, (64, 128), 1)
    gram[512:576, 512:640] = jnp.where(lane64 < 64, corner, 0.0)
    for s in range(4):
        for b in range(s, 5):
            if b == s:
                if s:
                    gram[128 * s : 128 * s + 128, 128 * s : 128 * s + 128] = packed[
                        STRIP[s] : STRIP[s] + 128, :
                    ]
                continue
            n = 64 if b == 4 else 128
            start = STRIP[s] + 128 * (b - s)
            block = packed[start : start + n, :]
            gram[128 * b : 128 * b + n, 128 * s : 128 * s + 128] = block
            if n == 64:
                block = jnp.concatenate([block, jnp.zeros((64, 128), F32)], axis=0)
            gram[128 * s : 128 * s + 128, 128 * b : 128 * b + 128] = block.T


def spread(count, factor, act):
    for i in range(1, 8):
        act((i * factor) % count)

    def block(b, carry):
        for i in range(8):
            act(jnp.bitwise_and((8 * b + i) * factor, count - 1))
        return carry

    lax.fori_loop(1, count // 8, block, 0)


def greet_all(me):
    barrier = pltpu.get_barrier_semaphore()

    def greet(mask):
        pl.semaphore_signal(
            barrier, inc=1, device_id=(jnp.bitwise_xor(me, mask),), device_id_type=MESH
        )

    spread(DEVICES, 45, greet)
    return lambda: pl.semaphore_wait(barrier, DEVICES - 1)


def place_at(chip):
    return {"y": chip // 16, "z": lax.rem(chip // 4, 4), "x": lax.rem(chip, 4)}


def shift(at, axis, step):
    moved = dict(at)
    moved[axis] = lax.rem(at[axis] + step + 4, 4)
    return moved


def device_at(at, core):
    return ((at["y"] * 4 + at["z"]) * 4 + at["x"]) * 2 + core


def left_form(value, ref):
    high, low = split(value)
    tail = value[:, 512:RP]
    ref[:, 0:512] = high[:, 0:512]
    ref[:, 512:1024] = high[:, 0:512]
    ref[:, 1024:1536] = low[:, 0:512]
    ref[:, 1536:1664] = (tail + pltpu.roll(tail, 64, 1)).astype(BF16)
    ref[:, 1664:1792] = low[:, 512:RP]


def right_form(value, ref):
    high, low = split(value)
    ref[0:512, :] = high[0:512]
    ref[512:1024, :] = low[0:512]
    ref[1024:1536, :] = high[0:512]
    ref[1536:1600, :] = high[512:R]
    ref[1600:1664, :] = low[512:R]
    ref[1664:1728, :] = high[512:R]


def symmetric_dot(left, right, out):
    c0 = dot(left[...], right[:, 0:256])
    c1 = dot(left[256:R, :], right[:, 256:512])
    c2 = dot(left[512:R, :], right[:, 512:RP])
    blank = jnp.zeros((64, 256), F32)
    out[:, 0:256] = c0
    out[256:R, 256:512] = c1
    out[512:R, 512:RP] = c2
    out[0:256, 256:512] = c0[256:512].T
    out[0:256, 512:RP] = jnp.concatenate([c0[512:R], blank], axis=0).T
    out[256:512, 512:RP] = jnp.concatenate([c1[256:320], blank], axis=0).T


ORDERS = ("xyz", "yzx", "zxy")
OFFSETS = (0, -1, 1, 2)
SIDES = ((0, 1), (1, -1))


def gather_steps(buf, send_a, send_b, recv_a, recv_b, sib_send, sib_recv, meanwhile):
    me, chip, core = position()
    home = place_at(chip)
    sibling = chip * 2 + 1 - core
    parts = range(3)

    def device(at):
        return device_at(at, core)

    def rows_of(part, half):
        row = R * core + 192 * part + (0 if half is None else 96 * half)
        return pl.ds(pl.multiple_of(row, 16), 192 if half is None else 96)

    def tile(part, at):
        y, z, x = at["y"], at["z"], at["x"]
        return jnp.logical_or(y < 3, z < 2), 1, 0, lambda n: (y, z, pl.ds(x, n))

    def line(part, at):
        y, z, x = at["y"], at["z"], at["x"]
        if part == 0:
            return jnp.logical_or(y < 3, z < 2), 4, 0, lambda n: (y, z, pl.ds(0, n))
        if part == 1:
            return z < 2, 4, 3, lambda n: (pl.ds(0, n), z, x)
        return y < 3, 4, 2, lambda n: (y, pl.ds(0, n), x)

    def each(spec, act):
        whole, count, fewer, index = spec

        @pl.when(whole)
        def _():
            act(count, index(count))

        if fewer:

            @pl.when(jnp.logical_not(whole))
            def _():
                act(fewer, index(fewer))

    def push(part, spec, send_sem, recv_sem, to, half=None):
        def act(count, index):
            block = buf.at[(*index, rows_of(part, half))]
            remote(block, block, send_sem, recv_sem, to).start()

        each(spec, act)

    def take(spec, sem, rows=192):
        def act(count, index):
            drain(buf.at[0, 0, pl.ds(0, count), pl.ds(0, rows)], sem)

        each(spec, act)

    def take_halves(first, second, sem):
        def outer(m, _):
            def inner(n, _):
                drain(buf.at[0, 0, 0, pl.ds(0, 96 * (m + n))], sem)

            each(second, inner)
            if not second[2]:

                @pl.when(jnp.logical_not(second[0]))
                def _():
                    drain(buf.at[0, 0, 0, pl.ds(0, 96 * m)], sem)

        each(first, outer)
        if not first[2]:

            @pl.when(jnp.logical_and(jnp.logical_not(first[0]), second[0]))
            def _():
                drain(buf.at[0, 0, 0, pl.ds(0, 96 * second[1])], sem)

    def both(part, k, spec, axis):
        for d, step in SIDES:
            push(part, spec, send_a.at[part, k], recv_a.at[part, k, d], device(shift(home, axis, step)))

    def pass_on(part, k, spec, d, axis, step):
        push(part, spec, send_b.at[part, k], recv_b.at[part, k], device(shift(home, axis, step)), half=d)

    def near(part, axis, step, i):
        return line(part, shift(shift(home, axis, step), ORDERS[part][1], OFFSETS[i]))

    def tell(part, spec):
        push(part, spec, sib_send, sib_recv, sibling)

    def forward(part, i):
        axis = ORDERS[part][2]
        for d, step in SIDES:
            got = near(part, axis, -step, i)
            take(got, recv_a.at[part, 2 + i, d])
            pass_on(part, 2 + i, got, d, axis, step)
            tell(part, got)

    for p in parts:
        own, axis = tile(p, home), ORDERS[p][0]
        both(p, 0, own, axis)
        push(p, own, send_a.at[p, 0], recv_b.at[p, 0], device(shift(home, axis, 2)))
    meanwhile()
    for p in parts:
        first, second, _ = ORDERS[p]
        for d, step in SIDES:
            take(tile(p, shift(home, first, -step)), recv_a.at[p, 0, d])
        take(tile(p, shift(home, first, 2)), recv_b.at[p, 0])
        both(p, 1, line(p, home), second)
    for p in parts:
        both(p, 2, line(p, home), ORDERS[p][2])
        tell(p, line(p, home))
    for p in parts:
        second = ORDERS[p][1]
        for d, step in SIDES:
            got = line(p, shift(home, second, -step))
            take(got, recv_a.at[p, 1, d])
            pass_on(p, 1, got, d, second, step)
    for p in parts:
        _, second, third = ORDERS[p]
        for d, step in SIDES:
            got = line(p, shift(home, second, -step))
            both(p, 3 + d, got, third)
            tell(p, got)
    for p in parts:
        forward(p, 0)
    for p in parts:
        _, second, third = ORDERS[p]
        got = line(p, shift(home, second, 2))
        take(got, recv_b.at[p, 1])
        both(p, 5, got, third)
        tell(p, got)
    for i in (1, 2, 3):
        for p in parts:
            forward(p, i)
    for p in parts:
        first, second, third = ORDERS[p]
        take(tile(p, home), send_a.at[p, 0], 576)
        take(line(p, home), send_a.at[p, 1], 384)
        take_halves(line(p, shift(home, second, -1)), line(p, shift(home, second, 1)), send_b.at[p, 1])
        for i in range(4):
            take(near(p, third, 0, i), send_a.at[p, 2 + i], 384)
    for i in range(4):
        for p in parts:
            got = near(p, ORDERS[p][2], 2, i)
            take(got, recv_b.at[p, 2 + i])
            tell(p, got)

    for p in parts:
        third = ORDERS[p][2]
        for i in range(4):
            take_halves(near(p, third, -1, i), near(p, third, 1, i), send_b.at[p, 2 + i])
    for sem in (sib_send, sib_recv):
        drain(buf.at[pl.ds(0, 3), :, :, pl.ds(0, 672)], sem)


def step_kernel(
    rows_ref, mom_ref, table_ref, fresh_ref, buf,
    wide, pieces, hits, outgoing, slot_row, slots, got, place, columns, packed, terms, partial, terms2, summed, relay, chosen, arrived, mcol,
    gram, gram2, ga, gb, pbs, ta, xa,
    a2a_send, a2a_recv, swap_send, swap_recv, rs1_send, rs2_send, ag1_send, ag2_send,
    h1_send, h1_recv, h2_send, h2_recv, sib_send, sib_recv, slot_sem,
    rs1_recv, rs2_recv, ag1_recv, ag2_recv, send_a, send_b, recv_b, recv_a,
):
    me, chip, core = position()
    greeted = greet_all(me)

    table = table_ref[...].astype(F32)
    owners = jnp.broadcast_to(table, (DEVICES, DEVICES))
    sub = lax.broadcasted_iota(jnp.int32, (DEVICES, DEVICES), 0)
    lane = lax.broadcasted_iota(jnp.int32, (DEVICES, DEVICES), 1)
    earlier = jnp.logical_and(owners == owners.T, sub < lane)
    rank = jnp.sum(jnp.where(earlier, 1.0, 0.0), axis=0, keepdims=True)
    slot_row[...] = (3.0 * table + rank).astype(jnp.int32)
    slot_copy = pltpu.make_async_copy(slot_row, slots, slot_sem)
    slot_copy.start()
    owned = jnp.sum(jnp.where(table == me.astype(F32), 1.0, 0.0), axis=1, keepdims=True)
    line = (16.0 * table + 5.0 * rank).astype(jnp.int32)
    lines = lax.broadcasted_iota(jnp.int32, (16 * DEVICES, DEVICES), 0)
    for i in range(5):
        hits[:, 128 * i : 128 * i + 128] = jnp.where(lines == line + i, 1.0, 0.0).astype(BF16)
    wide[...] = jnp.zeros_like(wide)
    for i in range(9):
        wide[i, :, 0:56] = rows_ref[i].astype(F32)
    for i in range(5):
        pair = wide[2 * i] + pltpu.roll(wide[2 * i + 1], 64, 1)
        pieces[128 * i : 128 * i + 128, :] = pair.astype(BF16)
    outgoing[...] = dot(hits[...], pieces[...]).astype(BF16).reshape(DEVICES, 16, 128)
    slot_copy.wait()
    greeted()


    def push(mask):
        to = jnp.bitwise_xor(me, mask)
        remote(outgoing.at[to], got.at[me], a2a_send, a2a_recv, to).start()

    spread(DEVICES, 45, push)
    got[pl.ds(me, 1)] = outgoing[pl.ds(me, 1)]
    rows = lax.broadcasted_iota(jnp.int32, (256, 128), 0)
    lanes = lax.broadcasted_iota(jnp.int32, (1, 128), 1)
    for t in range(9):
        row = lanes + 128 * t
        source = lax.shift_right_logical(row * 7282, 16)
        r = row - 9 * source
        half = lax.shift_right_logical(r, 1)
        odd = r - 2 * half
        base = 16 * (source - window_start(t)) + half
        for k in range(3):
            for parity in range(2):
                target = jnp.where(odd == parity, base + 5 * k, -1)
                place[t, :, pl.ds(128 * (2 * k + parity), 128)] = jnp.where(
                    rows == target, 1.0, 0.0
                ).astype(BF16)
    for i in range(ITERS - 1):
        pbs[i, 1728:K3, :] = jnp.zeros((K3 - 1728, RP), BF16)
    gb[1728:K3, :] = jnp.zeros((K3 - 1728, RP), BF16)
    chosen[DEVICES : DEVICES + 2] = jnp.zeros((2, 8, 128), F32)
    others = got.at[pl.ds(0, DEVICES - 1)]
    drain(others, a2a_recv)
    for t in range(9):
        window = got[pl.ds(window_start(t), 16)].reshape(256, 128)
        placed = lax.dot_general(
            window, place[t], (((0,), (0,)), ((), ())), preferred_element_type=F32
        )
        for k in range(3):
            grad = (
                placed[0:56, 256 * k : 256 * k + 128]
                + placed[64:120, 256 * k + 128 : 256 * k + 256]
            )
            fresh_ref[k, :, pl.ds(128 * t, 128)] = (
                0.95 * mom_ref[k, :, pl.ds(128 * t, 128)] + grad
            ) * jnp.where(owned > k, 1.0, 0.0)

    sibling = chip * 2 + 1 - core
    mine_lanes = pl.ds(pl.multiple_of(512 * core, 128), RP)
    their_lanes = pl.ds(pl.multiple_of(512 * (1 - core), 128), RP)
    swap = remote(fresh_ref.at[:, :, their_lanes], columns.at[1], swap_send, swap_recv, sibling)
    swap.start()
    columns[0] = fresh_ref[:, :, mine_lanes]
    swap.wait_recv()
    both = align_layer(columns[...].reshape(336, RP), core)
    high, low = split(both)
    gram[...] = lax.dot_general(
        jnp.concatenate([high, high, low], axis=0),
        jnp.concatenate([high, low, high], axis=0),
        (((0,), (0,)), ((), ())),
        preferred_element_type=F32,
    )[0:R]
    pack(gram, packed)

    home = place_at(chip)

    def plane_of(p):
        return home[ORDERS[p][0]] * 4 + home[ORDERS[p][1]]

    def block_of(p, third):
        return pl.ds(pl.multiple_of(512 * p + 128 * third, 8), 128)

    def piece_of(p, plane):
        return pl.ds(pl.multiple_of(512 * p + 128 * home[ORDERS[p][2]] + 8 * plane, 8), 8)

    def plane_peer(p, mask):
        other = jnp.bitwise_xor(plane_of(p), mask)
        at = dict(home)
        at[ORDERS[p][0]] = other // 4
        at[ORDERS[p][1]] = lax.rem(other, 4)
        return other, device_at(at, core)

    for p in range(3):
        third = ORDERS[p][2]
        for step in (1, 2, 3):
            there = shift(home, third, step)
            remote(
                packed.at[block_of(p, there[third])],
                terms.at[p, home[third]],
                rs1_send, rs1_recv.at[p], device_at(there, core),
            ).start()
    for p in range(3):
        third = home[ORDERS[p][2]]
        terms[p, pl.ds(third, 1)] = packed[block_of(p, third)][None]
        drain(packed.at[pl.ds(0, 384)], rs1_recv.at[p])
        partial[p] = jnp.sum(terms[p], axis=0)
        for mask in range(1, 16):
            other, to = plane_peer(p, mask)
            remote(
                partial.at[p, pl.ds(pl.multiple_of(8 * other, 8), 8)],
                terms2.at[p, plane_of(p)],
                rs2_send, rs2_recv.at[p], to,
            ).start()
    for p in range(3):
        plane = plane_of(p)
        terms2[p, pl.ds(plane, 1)] = partial[p, pl.ds(pl.multiple_of(8 * plane, 8), 8)][None]
        drain(packed.at[pl.ds(0, 120)], rs2_recv.at[p])
        summed[piece_of(p, plane)] = jnp.sum(terms2[p], axis=0)
        for mask in range(1, 16):
            _, to = plane_peer(p, mask)
            piece = summed.at[piece_of(p, plane)]
            remote(piece, piece, ag1_send, ag1_recv.at[p], to).start()
    for p in range(3):
        third = ORDERS[p][2]
        drain(packed.at[pl.ds(0, 120)], ag1_recv.at[p])
        block = summed.at[block_of(p, home[third])]
        for step in (1, 2, 3):
            remote(block, block, ag2_send, ag2_recv.at[p], device_at(shift(home, third, step), core)).start()

    def to_relay(n, carry):
        i = lax.rem(n + 28, RELAYS)
        t = i // 7
        q = lax.rem(i, 7)
        to = jnp.where(i < 28, 2 * i + 1, jnp.where(i < 35, 2 * i + 57, 2 * i - 14))
        src = fresh_ref.at[
            :, pl.ds(pl.multiple_of(8 * q, 8), 8), pl.ds(pl.multiple_of(128 * t, 128), 128)
        ]
        dst = relay.at[pl.ds(3 * me, 3)]

        @pl.when(to != me)
        def _():
            remote(src, dst, h1_send, h1_recv, to).start()

        @pl.when(to == me)
        def _():
            pltpu.make_async_copy(src, dst, h1_recv).start()

        return carry

    lax.fori_loop(0, RELAYS, to_relay, 0, unroll=7)

    for p in range(3):
        drain(packed.at[pl.ds(0, 384)], ag2_recv.at[p])
    unpack(summed, gram)
    spans = jnp.logical_and(core == 1, jnp.logical_and(chip >= 56, chip < 63))
    sole = jnp.where(core == 1, chip < 28, jnp.logical_and(chip >= 28, chip < 56))
    relays = jnp.logical_or(spans, sole)
    u = jnp.where(core == 1, jnp.where(chip < 28, chip, chip - 28), chip + 7)
    lane_tile = u // 7 - 4 * (1 - core)
    q = lax.rem(u, 7)

    def first_block(j, q):
        return (16 * j - q + 6) // 7

    def relay_blocks():
        drain(relay, h1_recv)

        def choose(b, carry):
            chosen[pl.ds(b, 1)] = relay[pl.ds(jnp.clip(slots[0, b], 0, 383), 1)]
            return carry

        lax.fori_loop(0, DEVICES, choose, 0, unroll=8)

    def send_columns(tile, layer):
        def to_columns(j, carry):
            src = chosen.at[pl.ds(first_block(j, q), 3)]
            remote(src, arrived.at[tile, q], h2_send, h2_recv, j * 2 + layer).start()
            return carry

        lax.fori_loop(0, TILES, to_columns, 0, unroll=8)

    @pl.when(spans)
    def _():
        relay_blocks()
        send_columns(4, 0)
        send_columns(0, 1)

    diag = lax.broadcasted_iota(jnp.int32, (R, RP), 0) == lax.broadcasted_iota(jnp.int32, (R, RP), 1)
    squares = jnp.sum(jnp.where(diag, gram[...], 0.0), axis=(0, 1), keepdims=True)
    inverse = 1.0 / (jnp.sqrt(squares) + epsilon)
    gram[...] = gram[...] * (inverse * inverse)

    def polynomial(i):
        g = gram[...]
        left_form(g, ga)
        right_form(g, gb)
        symmetric_dot(ga, gb, gram2)
        p = coef_b * g + coef_c * gram2[...]
        right_form(jnp.where(diag, p + coef_a, p), pbs.at[i])

    def sweep(i, carry):
        polynomial(i)
        symmetric_dot(ga, pbs.at[i], gram2)
        left_form(gram2[...], ta)
        symmetric_dot(ta, pbs.at[i], gram)
        return carry

    lax.fori_loop(0, 2, sweep, 0)

    @pl.when(sole)
    def _():
        relay_blocks()
        send_columns(lane_tile, 1 - core)

    lax.fori_loop(2, ITERS - 1, sweep, 0)
    right_form(gram[...], gb)

    @pl.when(chip < TILES)
    def _():
        drain(arrived, h2_recv)
        for i in range(16):
            octet = 16 * chip + i
            block = octet // 7
            r = octet - 7 * block
            for t in range(5):
                mcol[8 * i : 8 * i + 8, 128 * t : 128 * t + 128] = arrived[
                    t, r, block - first_block(chip, r)
                ]

    @pl.when(chip >= TILES)
    def _():
        mcol[...] = jnp.zeros_like(mcol)

    value = align_layer(mcol[...], core) * inverse

    def apply(i, value):
        left_form(value, xa)
        return dot(xa[...], pbs[i])

    value = lax.fori_loop(0, ITERS - 1, apply, value)
    left_form(value, xa)
    once = dot(xa[...], gb[...])
    left_form(once, xa)
    twice = dot(xa[...], gb[...])
    value = (coef_a * value + coef_b * once + coef_c * twice) * (0.2 * math.sqrt(max(R, 7168)))
    buf[chip // 16, lax.rem(chip // 4, 4), lax.rem(chip, 4), pl.ds(pl.multiple_of(R * core, 16), R)] = (
        value.T[0:R, :].astype(BF16)
    )
    def earlier_sent():
        drain(others, a2a_send)
        swap.wait_send()
        drain(packed.at[pl.ds(0, 1152)], rs1_send)
        drain(packed.at[pl.ds(0, 360)], rs2_send)
        drain(packed.at[pl.ds(0, 360)], ag1_send)
        drain(packed.at[pl.ds(0, 1152)], ag2_send)

        @pl.when(relays)
        def _():
            drain(relay.at[pl.ds(0, 3 * (RELAYS - 1))], h1_send)

        @pl.when(jnp.logical_not(relays))
        def _():
            drain(relay.at[pl.ds(0, 3 * RELAYS)], h1_send)

        @pl.when(sole)
        def _():
            drain(relay.at[pl.ds(0, 3 * TILES)], h2_send)

        @pl.when(spans)
        def _():
            drain(relay.at[pl.ds(0, 6 * TILES)], h2_send)

    gather_steps(buf, send_a, send_b, recv_a, recv_b, sib_send, sib_recv, earlier_sent)


def step(rows, momentum, table):
    return pl.pallas_call(
        step_kernel,
        out_shape=(
            pltpu.VMEM(momentum.shape, F32),
            pltpu.VMEM((4, 4, 4, 2 * R, 128), BF16),
        ),
        in_specs=[
            pl.BlockSpec(memory_space=pltpu.VMEM),
            pl.BlockSpec(memory_space=pltpu.VMEM),
            pl.BlockSpec(memory_space=pltpu.VMEM),
        ],
        out_specs=(
            pl.BlockSpec(memory_space=pltpu.VMEM),
            pl.BlockSpec(memory_space=pltpu.VMEM),
        ),
        scratch_shapes=[
            pltpu.VMEM((10, 128, 128), F32),
            pltpu.VMEM((640, 128), BF16),
            pltpu.VMEM((16 * DEVICES, 5 * 128), BF16),
            pltpu.VMEM((DEVICES, 16, 128), BF16),
            pltpu.VMEM((1, DEVICES), jnp.int32),
            pltpu.SMEM((1, DEVICES), jnp.int32),
            pltpu.VMEM((DEVICES, 16, 128), BF16),
            pltpu.VMEM((9, 256, 768), BF16),
            pltpu.VMEM((2, 3, 56, RP), F32),
            pltpu.VMEM((1536, 128), F32),
            pltpu.VMEM((3, 4, 128, 128), F32),
            pltpu.VMEM((3, 128, 128), F32),
            pltpu.VMEM((3, 16, 8, 128), F32),
            pltpu.VMEM((1536, 128), F32),
            pltpu.VMEM((384, 8, 128), F32),
            pltpu.VMEM((DEVICES + 2, 8, 128), F32),
            pltpu.VMEM((5, 7, 3, 8, 128), F32),
            pltpu.VMEM((128, RP), F32),
            pltpu.VMEM((R, RP), F32),
            pltpu.VMEM((R, RP), F32),
            pltpu.VMEM((R, K3), BF16),
            pltpu.VMEM((K3, RP), BF16),
            pltpu.VMEM((ITERS - 1, K3, RP), BF16),
            pltpu.VMEM((R, K3), BF16),
            pltpu.VMEM((128, K3), BF16),
        ]
        + [pltpu.SemaphoreType.DMA] * 15
        + [pltpu.SemaphoreType.DMA((3,))] * 4
        + [pltpu.SemaphoreType.DMA((3, 6))] * 3
        + [pltpu.SemaphoreType.DMA((3, 6, 2))],
        compiler_params=pltpu.CompilerParams(
            collective_id=0, has_side_effects=True, vmem_limit_bytes=40 * 2**20
        ),
        name="step",
    )(rows, momentum, table)


def place_kernel(buf, fresh, update, momentum, sem):
    copies = [
        pltpu.make_async_copy(
            buf.at[j // 16, j // 4 % 4, j % 4], update.at[:, pl.ds(128 * j, 128)], sem.at[j]
        )
        for j in range(TILES)
    ]
    copies.append(pltpu.make_async_copy(fresh, momentum, sem.at[TILES]))
    for copy in copies:
        copy.start()
    for copy in copies:
        copy.wait()


def place_results(buf, fresh):
    return pl.pallas_call(
        place_kernel,
        out_shape=(
            jax.ShapeDtypeStruct((2 * R, 128 * TILES), BF16),
            jax.ShapeDtypeStruct(fresh.shape, F32),
        ),
        in_specs=[pl.BlockSpec(memory_space=pl.ANY)] * 2,
        out_specs=(pl.BlockSpec(memory_space=pl.ANY),) * 2,
        scratch_shapes=[pltpu.SemaphoreType.DMA((TILES + 1,))],
        compiler_params=pltpu.CompilerParams(vmem_limit_bytes=2 * 2**20),
        name="place",
    )(buf, fresh)


def local(grads, momentum, table):
    fresh, buf = step(grads.reshape(9, 128, 56), momentum, table.reshape(1, DEVICES))
    return place_results(buf, fresh)


def solution(mesh):
    in_specs = (P("dp", None), P("dp", None, None), P())
    out_specs = (P(), P("dp", None, None))
    return jax.shard_map(local, mesh=mesh, in_specs=in_specs, out_specs=out_specs, check_vma=False)
```

```python
import math

import jax
import jax.numpy as jnp
from jax import lax
from jax.experimental import pallas as pl
from jax.experimental.pallas import tpu as pltpu
from jax.sharding import PartitionSpec as P

R = 576
ITERS = 5
RP = 640
K3 = 1792
DEVICES = 128
CHIPS = 64
TILES = 56
RELAYS = 63
MESH = pl.DeviceIdType.MESH
F32 = jnp.float32
BF16 = jnp.bfloat16

coef_a = 3.4445
coef_b = -4.775
coef_c = 2.0315
epsilon = 1e-07


def position():
    me = lax.axis_index("dp")
    return me, me // 2, lax.rem(me, 2)


def remote(src, dst, send, recv, to):
    return pltpu.make_async_remote_copy(
        src, dst, send, recv, device_id=(to,), device_id_type=MESH
    )


def drain(view, sem):
    pltpu.make_async_copy(view, view, sem).wait()


def split(value):
    high = value.astype(BF16)
    return high, (value - high.astype(F32)).astype(BF16)


def dot(a, b):
    return jnp.dot(a, b, preferred_element_type=F32)


def window_start(t):
    return min(128 * t // 9, DEVICES - 16)


def align_layer(value, core):
    moved = pltpu.roll(value, (RP - 64) * core, 1)
    lane = lax.broadcasted_iota(jnp.int32, value.shape, 1)
    return jnp.where(lane < R, moved, 0.0)


STRIP = (0, 576, 1024, 1344)


def pack(gram, packed):
    lane = lax.broadcasted_iota(jnp.int32, (64, 128), 1)
    corner = pltpu.roll(gram[512:576, 512:640], 64, 1)
    packed[0:64, :] = jnp.where(lane < 64, gram[0:64, 0:128], corner)
    packed[64:576, :] = gram[64:576, 0:128]
    for s in range(1, 4):
        packed[STRIP[s] : STRIP[s] + 576 - 128 * s, :] = gram[
            128 * s : 576, 128 * s : 128 * s + 128
        ]


def unpack(packed, gram):
    row = lax.broadcasted_iota(jnp.int32, (128, 128), 0)
    lane = lax.broadcasted_iota(jnp.int32, (128, 128), 1)
    upper = (row < 64) & (lane >= 64)
    first = packed[0:128, :]
    clean = jnp.where(upper, 0.0, first)
    gram[0:128, 0:128] = jnp.where(upper, clean.T, clean)
    corner = pltpu.roll(packed[0:64, :], 64, 1)
    lane64 = lax.broadcasted_iota(jnp.int32, (64, 128), 1)
    gram[512:576, 512:640] = jnp.where(lane64 < 64, corner, 0.0)
    for s in range(4):
        for b in range(s, 5):
            if b == s:
                if s:
                    gram[128 * s : 128 * s + 128, 128 * s : 128 * s + 128] = packed[
                        STRIP[s] : STRIP[s] + 128, :
                    ]
                continue
            n = 64 if b == 4 else 128
            start = STRIP[s] + 128 * (b - s)
            block = packed[start : start + n, :]
            gram[128 * b : 128 * b + n, 128 * s : 128 * s + 128] = block
            if n == 64:
                block = jnp.concatenate([block, jnp.zeros((64, 128), F32)], axis=0)
            gram[128 * s : 128 * s + 128, 128 * b : 128 * b + 128] = block.T


def spread(count, factor, act):
    for i in range(1, 8):
        act((i * factor) % count)

    def block(b, carry):
        for i in range(8):
            act(jnp.bitwise_and((8 * b + i) * factor, count - 1))
        return carry

    lax.fori_loop(1, count // 8, block, 0)


def greet_all(me):
    barrier = pltpu.get_barrier_semaphore()

    def greet(mask):
        pl.semaphore_signal(
            barrier, inc=1, device_id=(jnp.bitwise_xor(me, mask),), device_id_type=MESH
        )

    spread(DEVICES, 45, greet)
    return lambda: pl.semaphore_wait(barrier, DEVICES - 1)


def place_at(chip):
    return {"y": chip // 16, "z": lax.rem(chip // 4, 4), "x": lax.rem(chip, 4)}


def shift(at, axis, step):
    moved = dict(at)
    moved[axis] = lax.rem(at[axis] + step + 4, 4)
    return moved


def device_at(at, core):
    return ((at["y"] * 4 + at["z"]) * 4 + at["x"]) * 2 + core


def left_form(value, ref):
    high, low = split(value)
    tail = value[:, 512:RP]
    ref[:, 0:512] = high[:, 0:512]
    ref[:, 512:1024] = high[:, 0:512]
    ref[:, 1024:1536] = low[:, 0:512]
    ref[:, 1536:1664] = (tail + pltpu.roll(tail, 64, 1)).astype(BF16)
    ref[:, 1664:1792] = low[:, 512:RP]


def right_form(value, ref):
    high, low = split(value)
    ref[0:512, :] = high[0:512]
    ref[512:1024, :] = low[0:512]
    ref[1024:1536, :] = high[0:512]
    ref[1536:1600, :] = high[512:R]
    ref[1600:1664, :] = low[512:R]
    ref[1664:1728, :] = high[512:R]


def symmetric_dot(left, right, out):
    c0 = dot(left[...], right[:, 0:256])
    c1 = dot(left[256:R, :], right[:, 256:512])
    c2 = dot(left[512:R, :], right[:, 512:RP])
    blank = jnp.zeros((64, 256), F32)
    out[:, 0:256] = c0
    out[256:R, 256:512] = c1
    out[512:R, 512:RP] = c2
    out[0:256, 256:512] = c0[256:512].T
    out[0:256, 512:RP] = jnp.concatenate([c0[512:R], blank], axis=0).T
    out[256:512, 512:RP] = jnp.concatenate([c1[256:320], blank], axis=0).T


ORDERS = ("xyz", "yzx", "zxy")
OFFSETS = (0, -1, 1, 2)
SIDES = ((0, 1), (1, -1))


def gather_steps(buf, send_a, send_b, recv_a, recv_b, sib_send, sib_recv, meanwhile):
    me, chip, core = position()
    home = place_at(chip)
    sibling = chip * 2 + 1 - core
    parts = range(3)

    def device(at):
        return device_at(at, core)

    def rows_of(part, half):
        row = R * core + 192 * part + (0 if half is None else 96 * half)
        return pl.ds(pl.multiple_of(row, 16), 192 if half is None else 96)

    def tile(part, at):
        y, z, x = at["y"], at["z"], at["x"]
        return jnp.logical_or(y < 3, z < 2), 1, 0, lambda n: (y, z, pl.ds(x, n))

    def line(part, at):
        y, z, x = at["y"], at["z"], at["x"]
        if part == 0:
            return jnp.logical_or(y < 3, z < 2), 4, 0, lambda n: (y, z, pl.ds(0, n))
        if part == 1:
            return z < 2, 4, 3, lambda n: (pl.ds(0, n), z, x)
        return y < 3, 4, 2, lambda n: (y, pl.ds(0, n), x)

    def each(spec, act):
        whole, count, fewer, index = spec

        @pl.when(whole)
        def _():
            act(count, index(count))

        if fewer:

            @pl.when(jnp.logical_not(whole))
            def _():
                act(fewer, index(fewer))

    def push(part, spec, send_sem, recv_sem, to, half=None):
        def act(count, index):
            block = buf.at[(*index, rows_of(part, half))]
            remote(block, block, send_sem, recv_sem, to).start()

        each(spec, act)

    def take(spec, sem, rows=192):
        def act(count, index):
            drain(buf.at[0, 0, pl.ds(0, count), pl.ds(0, rows)], sem)

        each(spec, act)

    def take_halves(first, second, sem):
        def outer(m, _):
            def inner(n, _):
                drain(buf.at[0, 0, 0, pl.ds(0, 96 * (m + n))], sem)

            each(second, inner)
            if not second[2]:

                @pl.when(jnp.logical_not(second[0]))
                def _():
                    drain(buf.at[0, 0, 0, pl.ds(0, 96 * m)], sem)

        each(first, outer)
        if not first[2]:

            @pl.when(jnp.logical_and(jnp.logical_not(first[0]), second[0]))
            def _():
                drain(buf.at[0, 0, 0, pl.ds(0, 96 * second[1])], sem)

    def both(part, k, spec, axis):
        for d, step in SIDES:
            push(part, spec, send_a.at[part, k], recv_a.at[part, k, d], device(shift(home, axis, step)))

    def pass_on(part, k, spec, d, axis, step):
        push(part, spec, send_b.at[part, k], recv_b.at[part, k], device(shift(home, axis, step)), half=d)

    def near(part, axis, step, i):
        return line(part, shift(shift(home, axis, step), ORDERS[part][1], OFFSETS[i]))

    def tell(part, spec):
        push(part, spec, sib_send, sib_recv, sibling)

    def forward(part, i):
        axis = ORDERS[part][2]
        for d, step in SIDES:
            got = near(part, axis, -step, i)
            take(got, recv_a.at[part, 2 + i, d])
            pass_on(part, 2 + i, got, d, axis, step)
            tell(part, got)

    def finish(part, i):
        got = near(part, ORDERS[part][2], 2, i)
        take(got, recv_b.at[part, 2 + i])
        tell(part, got)

    for p in parts:
        own, axis = tile(p, home), ORDERS[p][0]
        both(p, 0, own, axis)
        push(p, own, send_a.at[p, 0], recv_b.at[p, 0], device(shift(home, axis, 2)))
    meanwhile()
    for p in parts:
        first, second, _ = ORDERS[p]
        for d, step in SIDES:
            take(tile(p, shift(home, first, -step)), recv_a.at[p, 0, d])
        take(tile(p, shift(home, first, 2)), recv_b.at[p, 0])
        both(p, 1, line(p, home), second)
    for p in parts:
        both(p, 2, line(p, home), ORDERS[p][2])
        tell(p, line(p, home))
    for p in parts:
        second = ORDERS[p][1]
        for d, step in SIDES:
            got = line(p, shift(home, second, -step))
            take(got, recv_a.at[p, 1, d])
            pass_on(p, 1, got, d, second, step)
    for p in parts:
        _, second, third = ORDERS[p]
        for d, step in SIDES:
            got = line(p, shift(home, second, -step))
            both(p, 3 + d, got, third)
            tell(p, got)
    for p in parts:
        forward(p, 0)
    for p in parts:
        _, second, third = ORDERS[p]
        got = line(p, shift(home, second, 2))
        take(got, recv_b.at[p, 1])
        both(p, 5, got, third)
        tell(p, got)
    for i in (1, 2, 3):
        for p in parts:
            forward(p, i)
        if i > 1:
            for p in parts:
                finish(p, i - 2)
    for p in parts:
        first, second, third = ORDERS[p]
        take(tile(p, home), send_a.at[p, 0], 576)
        take(line(p, home), send_a.at[p, 1], 384)
        take_halves(line(p, shift(home, second, -1)), line(p, shift(home, second, 1)), send_b.at[p, 1])
        for i in range(4):
            take(near(p, third, 0, i), send_a.at[p, 2 + i], 384)
    for i in (2, 3):
        for p in parts:
            finish(p, i)

    for p in parts:
        third = ORDERS[p][2]
        for i in range(4):
            take_halves(near(p, third, -1, i), near(p, third, 1, i), send_b.at[p, 2 + i])
    for sem in (sib_send, sib_recv):
        drain(buf.at[pl.ds(0, 3), :, :, pl.ds(0, 672)], sem)


def step_kernel(
    rows_ref, mom_ref, table_ref, fresh_ref, buf,
    wide, pieces, hits, outgoing, slot_row, slots, got, place, columns, packed, terms, partial, terms2, summed, relay, chosen, arrived, mcol,
    gram, gram2, ga, gb, pbs, ta, xa,
    a2a_send, a2a_recv, swap_send, swap_recv, rs1_send, rs2_send, ag1_send, ag2_send,
    h1_send, h1_recv, h2_send, h2_recv, sib_send, sib_recv, slot_sem,
    rs1_recv, rs2_recv, ag1_recv, ag2_recv, send_a, send_b, recv_b, recv_a,
):
    me, chip, core = position()
    greeted = greet_all(me)

    table = table_ref[...].astype(F32)
    owners = jnp.broadcast_to(table, (DEVICES, DEVICES))
    sub = lax.broadcasted_iota(jnp.int32, (DEVICES, DEVICES), 0)
    lane = lax.broadcasted_iota(jnp.int32, (DEVICES, DEVICES), 1)
    earlier = jnp.logical_and(owners == owners.T, sub < lane)
    rank = jnp.sum(jnp.where(earlier, 1.0, 0.0), axis=0, keepdims=True)
    slot_row[...] = (3.0 * table + rank).astype(jnp.int32)
    slot_copy = pltpu.make_async_copy(slot_row, slots, slot_sem)
    slot_copy.start()
    owned = jnp.sum(jnp.where(table == me.astype(F32), 1.0, 0.0), axis=1, keepdims=True)
    line = (16.0 * table + 5.0 * rank).astype(jnp.int32)
    lines = lax.broadcasted_iota(jnp.int32, (16 * DEVICES, DEVICES), 0)
    for i in range(5):
        hits[:, 128 * i : 128 * i + 128] = jnp.where(lines == line + i, 1.0, 0.0).astype(BF16)
    wide[...] = jnp.zeros_like(wide)
    for i in range(9):
        wide[i, :, 0:56] = rows_ref[i].astype(F32)
    for i in range(5):
        pair = wide[2 * i] + pltpu.roll(wide[2 * i + 1], 64, 1)
        pieces[128 * i : 128 * i + 128, :] = pair.astype(BF16)
    outgoing[...] = dot(hits[...], pieces[...]).astype(BF16).reshape(DEVICES, 16, 128)
    slot_copy.wait()
    greeted()


    def push(mask):
        to = jnp.bitwise_xor(me, mask)
        remote(outgoing.at[to], got.at[me], a2a_send, a2a_recv, to).start()

    spread(DEVICES, 45, push)
    got[pl.ds(me, 1)] = outgoing[pl.ds(me, 1)]
    rows = lax.broadcasted_iota(jnp.int32, (256, 128), 0)
    lanes = lax.broadcasted_iota(jnp.int32, (1, 128), 1)
    for t in range(9):
        row = lanes + 128 * t
        source = lax.shift_right_logical(row * 7282, 16)
        r = row - 9 * source
        half = lax.shift_right_logical(r, 1)
        odd = r - 2 * half
        base = 16 * (source - window_start(t)) + half
        for k in range(3):
            for parity in range(2):
                target = jnp.where(odd == parity, base + 5 * k, -1)
                place[t, :, pl.ds(128 * (2 * k + parity), 128)] = jnp.where(
                    rows == target, 1.0, 0.0
                ).astype(BF16)
    for i in range(ITERS - 1):
        pbs[i, 1728:K3, :] = jnp.zeros((K3 - 1728, RP), BF16)
    gb[1728:K3, :] = jnp.zeros((K3 - 1728, RP), BF16)
    chosen[DEVICES : DEVICES + 2] = jnp.zeros((2, 8, 128), F32)
    others = got.at[pl.ds(0, DEVICES - 1)]
    drain(others, a2a_recv)
    for t in range(9):
        window = got[pl.ds(window_start(t), 16)].reshape(256, 128)
        placed = lax.dot_general(
            window, place[t], (((0,), (0,)), ((), ())), preferred_element_type=F32
        )
        for k in range(3):
            grad = (
                placed[0:56, 256 * k : 256 * k + 128]
                + placed[64:120, 256 * k + 128 : 256 * k + 256]
            )
            fresh_ref[k, :, pl.ds(128 * t, 128)] = (
                0.95 * mom_ref[k, :, pl.ds(128 * t, 128)] + grad
            ) * jnp.where(owned > k, 1.0, 0.0)

    sibling = chip * 2 + 1 - core
    mine_lanes = pl.ds(pl.multiple_of(512 * core, 128), RP)
    their_lanes = pl.ds(pl.multiple_of(512 * (1 - core), 128), RP)
    swap = remote(fresh_ref.at[:, :, their_lanes], columns.at[1], swap_send, swap_recv, sibling)
    swap.start()
    columns[0] = fresh_ref[:, :, mine_lanes]
    swap.wait_recv()
    both = align_layer(columns[...].reshape(336, RP), core)
    high, low = split(both)
    gram[...] = lax.dot_general(
        jnp.concatenate([high, high, low], axis=0),
        jnp.concatenate([high, low, high], axis=0),
        (((0,), (0,)), ((), ())),
        preferred_element_type=F32,
    )[0:R]
    pack(gram, packed)

    home = place_at(chip)

    def plane_of(p):
        return home[ORDERS[p][0]] * 4 + home[ORDERS[p][1]]

    def block_of(p, third):
        return pl.ds(pl.multiple_of(512 * p + 128 * third, 8), 128)

    def piece_of(p, plane):
        return pl.ds(pl.multiple_of(512 * p + 128 * home[ORDERS[p][2]] + 8 * plane, 8), 8)

    def plane_peer(p, mask):
        other = jnp.bitwise_xor(plane_of(p), mask)
        at = dict(home)
        at[ORDERS[p][0]] = other // 4
        at[ORDERS[p][1]] = lax.rem(other, 4)
        return other, device_at(at, core)

    for p in range(3):
        third = ORDERS[p][2]
        for step in (1, 2, 3):
            there = shift(home, third, step)
            remote(
                packed.at[block_of(p, there[third])],
                terms.at[p, home[third]],
                rs1_send, rs1_recv.at[p], device_at(there, core),
            ).start()
    for p in range(3):
        third = home[ORDERS[p][2]]
        terms[p, pl.ds(third, 1)] = packed[block_of(p, third)][None]
        drain(packed.at[pl.ds(0, 384)], rs1_recv.at[p])
        partial[p] = jnp.sum(terms[p], axis=0)
        for mask in range(1, 16):
            other, to = plane_peer(p, mask)
            remote(
                partial.at[p, pl.ds(pl.multiple_of(8 * other, 8), 8)],
                terms2.at[p, plane_of(p)],
                rs2_send, rs2_recv.at[p], to,
            ).start()
    for p in range(3):
        plane = plane_of(p)
        terms2[p, pl.ds(plane, 1)] = partial[p, pl.ds(pl.multiple_of(8 * plane, 8), 8)][None]
        drain(packed.at[pl.ds(0, 120)], rs2_recv.at[p])
        summed[piece_of(p, plane)] = jnp.sum(terms2[p], axis=0)
        for mask in range(1, 16):
            _, to = plane_peer(p, mask)
            piece = summed.at[piece_of(p, plane)]
            remote(piece, piece, ag1_send, ag1_recv.at[p], to).start()
    for p in range(3):
        third = ORDERS[p][2]
        drain(packed.at[pl.ds(0, 120)], ag1_recv.at[p])
        block = summed.at[block_of(p, home[third])]
        for step in (1, 2, 3):
            remote(block, block, ag2_send, ag2_recv.at[p], device_at(shift(home, third, step), core)).start()

    def to_relay(n, carry):
        i = lax.rem(n + 28, RELAYS)
        t = i // 7
        q = lax.rem(i, 7)
        to = jnp.where(i < 28, 2 * i + 1, jnp.where(i < 35, 2 * i + 57, 2 * i - 14))
        src = fresh_ref.at[
            :, pl.ds(pl.multiple_of(8 * q, 8), 8), pl.ds(pl.multiple_of(128 * t, 128), 128)
        ]
        dst = relay.at[pl.ds(3 * me, 3)]

        @pl.when(to != me)
        def _():
            remote(src, dst, h1_send, h1_recv, to).start()

        @pl.when(to == me)
        def _():
            pltpu.make_async_copy(src, dst, h1_recv).start()

        return carry

    lax.fori_loop(0, RELAYS, to_relay, 0, unroll=7)

    for p in range(3):
        drain(packed.at[pl.ds(0, 384)], ag2_recv.at[p])
    unpack(summed, gram)
    spans = jnp.logical_and(core == 1, jnp.logical_and(chip >= 56, chip < 63))
    sole = jnp.where(core == 1, chip < 28, jnp.logical_and(chip >= 28, chip < 56))
    relays = jnp.logical_or(spans, sole)
    u = jnp.where(core == 1, jnp.where(chip < 28, chip, chip - 28), chip + 7)
    lane_tile = u // 7 - 4 * (1 - core)
    q = lax.rem(u, 7)

    def first_block(j, q):
        return (16 * j - q + 6) // 7

    def relay_blocks():
        drain(relay, h1_recv)

        def choose(b, carry):
            chosen[pl.ds(b, 1)] = relay[pl.ds(jnp.clip(slots[0, b], 0, 383), 1)]
            return carry

        lax.fori_loop(0, DEVICES, choose, 0, unroll=8)

    def send_columns(tile, layer):
        def to_columns(j, carry):
            src = chosen.at[pl.ds(first_block(j, q), 3)]
            remote(src, arrived.at[tile, q], h2_send, h2_recv, j * 2 + layer).start()
            return carry

        lax.fori_loop(0, TILES, to_columns, 0, unroll=8)

    @pl.when(spans)
    def _():
        relay_blocks()
        send_columns(4, 0)
        send_columns(0, 1)

    diag = lax.broadcasted_iota(jnp.int32, (R, RP), 0) == lax.broadcasted_iota(jnp.int32, (R, RP), 1)
    squares = jnp.sum(jnp.where(diag, gram[...], 0.0), axis=(0, 1), keepdims=True)
    inverse = 1.0 / (jnp.sqrt(squares) + epsilon)
    gram[...] = gram[...] * (inverse * inverse)

    def polynomial(i):
        g = gram[...]
        left_form(g, ga)
        right_form(g, gb)
        symmetric_dot(ga, gb, gram2)
        p = coef_b * g + coef_c * gram2[...]
        right_form(jnp.where(diag, p + coef_a, p), pbs.at[i])

    def sweep(i, carry):
        polynomial(i)
        symmetric_dot(ga, pbs.at[i], gram2)
        left_form(gram2[...], ta)
        symmetric_dot(ta, pbs.at[i], gram)
        return carry

    lax.fori_loop(0, 2, sweep, 0)

    @pl.when(sole)
    def _():
        relay_blocks()
        send_columns(lane_tile, 1 - core)

    lax.fori_loop(2, ITERS - 1, sweep, 0)
    right_form(gram[...], gb)

    @pl.when(chip < TILES)
    def _():
        drain(arrived, h2_recv)
        for i in range(16):
            octet = 16 * chip + i
            block = octet // 7
            r = octet - 7 * block
            for t in range(5):
                mcol[8 * i : 8 * i + 8, 128 * t : 128 * t + 128] = arrived[
                    t, r, block - first_block(chip, r)
                ]

    @pl.when(chip >= TILES)
    def _():
        mcol[...] = jnp.zeros_like(mcol)

    value = align_layer(mcol[...], core) * inverse

    def apply(i, value):
        left_form(value, xa)
        return dot(xa[...], pbs[i])

    value = lax.fori_loop(0, ITERS - 1, apply, value)
    left_form(value, xa)
    once = dot(xa[...], gb[...])
    left_form(once, xa)
    twice = dot(xa[...], gb[...])
    value = (coef_a * value + coef_b * once + coef_c * twice) * (0.2 * math.sqrt(max(R, 7168)))
    buf[chip // 16, lax.rem(chip // 4, 4), lax.rem(chip, 4), pl.ds(pl.multiple_of(R * core, 16), R)] = (
        value.T[0:R, :].astype(BF16)
    )
    def earlier_sent():
        drain(others, a2a_send)
        swap.wait_send()
        drain(packed.at[pl.ds(0, 1152)], rs1_send)
        drain(packed.at[pl.ds(0, 360)], rs2_send)
        drain(packed.at[pl.ds(0, 360)], ag1_send)
        drain(packed.at[pl.ds(0, 1152)], ag2_send)

        @pl.when(relays)
        def _():
            drain(relay.at[pl.ds(0, 3 * (RELAYS - 1))], h1_send)

        @pl.when(jnp.logical_not(relays))
        def _():
            drain(relay.at[pl.ds(0, 3 * RELAYS)], h1_send)

        @pl.when(sole)
        def _():
            drain(relay.at[pl.ds(0, 3 * TILES)], h2_send)

        @pl.when(spans)
        def _():
            drain(relay.at[pl.ds(0, 6 * TILES)], h2_send)

    gather_steps(buf, send_a, send_b, recv_a, recv_b, sib_send, sib_recv, earlier_sent)


def step(rows, momentum, table):
    return pl.pallas_call(
        step_kernel,
        out_shape=(
            pltpu.VMEM(momentum.shape, F32),
            pltpu.VMEM((4, 4, 4, 2 * R, 128), BF16),
        ),
        in_specs=[
            pl.BlockSpec(memory_space=pltpu.VMEM),
            pl.BlockSpec(memory_space=pltpu.VMEM),
            pl.BlockSpec(memory_space=pltpu.VMEM),
        ],
        out_specs=(
            pl.BlockSpec(memory_space=pltpu.VMEM),
            pl.BlockSpec(memory_space=pltpu.VMEM),
        ),
        scratch_shapes=[
            pltpu.VMEM((10, 128, 128), F32),
            pltpu.VMEM((640, 128), BF16),
            pltpu.VMEM((16 * DEVICES, 5 * 128), BF16),
            pltpu.VMEM((DEVICES, 16, 128), BF16),
            pltpu.VMEM((1, DEVICES), jnp.int32),
            pltpu.SMEM((1, DEVICES), jnp.int32),
            pltpu.VMEM((DEVICES, 16, 128), BF16),
            pltpu.VMEM((9, 256, 768), BF16),
            pltpu.VMEM((2, 3, 56, RP), F32),
            pltpu.VMEM((1536, 128), F32),
            pltpu.VMEM((3, 4, 128, 128), F32),
            pltpu.VMEM((3, 128, 128), F32),
            pltpu.VMEM((3, 16, 8, 128), F32),
            pltpu.VMEM((1536, 128), F32),
            pltpu.VMEM((384, 8, 128), F32),
            pltpu.VMEM((DEVICES + 2, 8, 128), F32),
            pltpu.VMEM((5, 7, 3, 8, 128), F32),
            pltpu.VMEM((128, RP), F32),
            pltpu.VMEM((R, RP), F32),
            pltpu.VMEM((R, RP), F32),
            pltpu.VMEM((R, K3), BF16),
            pltpu.VMEM((K3, RP), BF16),
            pltpu.VMEM((ITERS - 1, K3, RP), BF16),
            pltpu.VMEM((R, K3), BF16),
            pltpu.VMEM((128, K3), BF16),
        ]
        + [pltpu.SemaphoreType.DMA] * 15
        + [pltpu.SemaphoreType.DMA((3,))] * 4
        + [pltpu.SemaphoreType.DMA((3, 6))] * 3
        + [pltpu.SemaphoreType.DMA((3, 6, 2))],
        compiler_params=pltpu.CompilerParams(
            collective_id=0, has_side_effects=True, vmem_limit_bytes=40 * 2**20
        ),
        name="step",
    )(rows, momentum, table)


def place_kernel(buf, fresh, update, momentum, sem):
    copies = [
        pltpu.make_async_copy(
            buf.at[j // 16, j // 4 % 4, j % 4], update.at[:, pl.ds(128 * j, 128)], sem.at[j]
        )
        for j in range(TILES)
    ]
    copies.append(pltpu.make_async_copy(fresh, momentum, sem.at[TILES]))
    for copy in copies:
        copy.start()
    for copy in copies:
        copy.wait()


def place_results(buf, fresh):
    return pl.pallas_call(
        place_kernel,
        out_shape=(
            jax.ShapeDtypeStruct((2 * R, 128 * TILES), BF16),
            jax.ShapeDtypeStruct(fresh.shape, F32),
        ),
        in_specs=[pl.BlockSpec(memory_space=pl.ANY)] * 2,
        out_specs=(pl.BlockSpec(memory_space=pl.ANY),) * 2,
        scratch_shapes=[pltpu.SemaphoreType.DMA((TILES + 1,))],
        compiler_params=pltpu.CompilerParams(vmem_limit_bytes=2 * 2**20),
        name="place",
    )(buf, fresh)


def local(grads, momentum, table):
    fresh, buf = step(grads.reshape(9, 128, 56), momentum, table.reshape(1, DEVICES))
    return place_results(buf, fresh)


def solution(mesh):
    in_specs = (P("dp", None), P("dp", None, None), P())
    out_specs = (P(), P("dp", None, None))
    return jax.shard_map(local, mesh=mesh, in_specs=in_specs, out_specs=out_specs, check_vma=False)
```
